256 devices in a mesh: fsdp: 32 (over y_hi, z, core), mp: 8 (over y_lo, x).
Axes of the slice: x: 4, y: 4 (y_hi: 2, y_lo: 2; y = y_hi * 2 + y_lo), z: 8, core: 2. Of those that a mesh axis runs over, the one named last changes fastest.
Arguments:
- tokens: bfloat16 [16384, 3072], P('fsdp', 'mp'), may hold values from -6 to 6
- ln_gain: float32 [3072], replicated, may hold values from 0.1 to 1.9
- w_qkv: bfloat16 [3072, 3, 3072], P('fsdp', None, 'mp'), may hold values from -0.109375 to 0.109375
- w_up: bfloat16 [3072, 12288], P('fsdp', 'mp'), may hold values from -0.109375 to 0.109375
- q_gain: float32 [24, 128], P('mp'), may hold values from 0.4 to 16
- k_gain: float32 [24, 128], P('mp'), may hold values from 0.4 to 16
- w_proj: bfloat16 [3072, 3072], P('mp', 'fsdp'), may hold values from -0.109375 to 0.109375
- w_down: bfloat16 [12288, 3072], P('mp', 'fsdp'), may hold values from -0.0546875 to 0.0546875
Outputs:
- block_out: bfloat16 [16384, 3072], P('fsdp', 'mp')
The draws below stay inside these ranges and needn't reach their ends.
All inputs are finite; a program needn't handle non-finite values.
Results may differ from the reference program's by a relative error of at most 0.015.
Values may be sent and summed in bfloat16 or wider, within the bound.
No kernel may reach another device: no remote copies, remote signals or barrier semaphores. Data moves between devices by JAX's collectives and lax.ppermute only.
A program may use at most 128 MiB of HBM per device.

```python
import jax
import jax.numpy as jnp
from jax import lax

H = 24
HD = 128
FF = 12288
PATCHES = 256
D = 3072
TOKENS = 16384
N_MP = 8


def draw_gain_table(key, low_head, high_head):
    head_key, entry_key = jax.random.split(key)
    head_scale = jnp.exp(jax.random.uniform(head_key, (H, 1), jnp.float32, jnp.log(low_head), jnp.log(high_head)))
    entries = jax.random.uniform(entry_key, (H, HD), jnp.float32, 0.6, 1.5)
    return entries * head_scale


def draw_q_gain(key, part):
    key = jax.random.fold_in(key, 11)
    return draw_gain_table(key, 0.8, 1.6)


def draw_k_gain(key, part):
    key = jax.random.fold_in(key, 23)
    return draw_gain_table(key, 0.8, 1.6)


def block_scale(rng, extent, pieces, smallest, high):
    loudness = 1.0
    for axis_at, blocks in pieces:
        heights = jax.random.uniform(jax.random.fold_in(jax.random.fold_in(rng, 6), axis_at), (blocks,), jnp.float32, smallest / len(pieces), high / len(pieces))
        loudness = loudness * jnp.repeat(jnp.exp(heights), extent[axis_at] // blocks).reshape((-1,) + (1,) * (len(extent) - 1 - axis_at))
    return loudness


def normal_values(own_key, extent, deviation, bound, cuts=(), kind=jnp.bfloat16):
    level = block_scale(own_key, extent, cuts, -0.22, 0.18) if cuts else 1.0
    values = jax.random.normal(own_key, extent, jnp.float32) * deviation * level
    return jnp.minimum(jnp.maximum(values, -bound), bound).astype(kind)


def setup_inputs(seed: int = 0) -> dict:
    key_of = jax.random.split(jax.random.key(seed), 9)
    return {
        "tokens": normal_values(key_of[0], (TOKENS, D), 1.0, 6.0, ((0, 32), (1, 8))),
        "ln_gain": jnp.clip(1.0 + 0.18 * jax.random.normal(key_of[1], (D,), jnp.float32), 0.1, 1.9),
        "w_qkv": normal_values(key_of[2], (D, 3, H * HD), D ** -0.5, 0.109375, ((0, 32), (2, 8))),
        "w_up": normal_values(key_of[3], (D, FF), D ** -0.5, 0.109375, ((0, 32), (1, 8))),
        "q_gain": draw_q_gain(jax.random.fold_in(key_of[8], 71), 0),
        "k_gain": draw_k_gain(jax.random.fold_in(key_of[8], 71), 0),
        "w_proj": normal_values(key_of[6], (H * HD, D), (H * HD) ** -0.5, 0.109375, ((0, 8), (1, 32))),
        "w_down": normal_values(key_of[7], (FF, D), FF ** -0.5, 0.0546875, ((0, 8), (1, 32))),
    }


def layer_norm(values, gain):
    mean = lax.optimization_barrier(jnp.mean(values, axis=-1, keepdims=True))
    centred = values - mean
    variance = lax.optimization_barrier(jnp.mean(centred * centred, axis=-1, keepdims=True))
    return centred * lax.rsqrt(variance + 1e-06) * gain

def one_image(inputs):
    queries, keys, values = inputs
    scores = jnp.einsum('qhd,khd->hqk', queries.astype(jnp.float32), keys.astype(jnp.float32)) * HD ** (-0.5)
    scores = scores - lax.optimization_barrier(jnp.max(scores, axis=-1, keepdims=True))
    weights = jnp.exp(scores)
    probs = (weights / lax.optimization_barrier(jnp.sum(weights, axis=-1, keepdims=True))).astype(jnp.bfloat16)
    mixed = jnp.einsum('hqk,khd->qhd', probs.astype(jnp.float32), values.astype(jnp.float32))
    return mixed.astype(jnp.bfloat16)

def reference(tokens, ln_gain, w_qkv, w_up, q_gain, k_gain, w_proj, w_down):
    rows = tokens.astype(jnp.float32)
    normed = layer_norm(rows, ln_gain).astype(jnp.bfloat16)
    projected = jnp.einsum('td,dca->cta', normed.astype(jnp.float32), w_qkv.astype(jnp.float32))
    images = TOKENS // PATCHES
    queries = layer_norm(projected[0].reshape(TOKENS, H, HD), q_gain).astype(jnp.bfloat16)
    keys = layer_norm(projected[1].reshape(TOKENS, H, HD), k_gain).astype(jnp.bfloat16)
    values = projected[2].reshape(TOKENS, H, HD).astype(jnp.bfloat16)
    attended = lax.map(one_image, (queries.reshape(images, PATCHES, H, HD), keys.reshape(images, PATCHES, H, HD), values.reshape(images, PATCHES, H, HD)))
    attended = attended.reshape(TOKENS, H * HD)
    hidden_pre = jnp.dot(normed, w_up, preferred_element_type=jnp.float32)
    activated = jax.nn.gelu(hidden_pre, approximate=False).astype(jnp.bfloat16)
    width_attn = H * HD // N_MP
    width_mlp = FF // N_MP
    branches = jnp.zeros((TOKENS, D), jnp.float32)
    for group in range(N_MP):
        term = jnp.dot(attended[:, group * width_attn:(group + 1) * width_attn], w_proj[group * width_attn:(group + 1) * width_attn], preferred_element_type=jnp.float32)
        term = term + jnp.dot(activated[:, group * width_mlp:(group + 1) * width_mlp], w_down[group * width_mlp:(group + 1) * width_mlp], preferred_element_type=jnp.float32)
        rounded = lax.optimization_barrier(term.astype(jnp.bfloat16))
        branches = branches + rounded.astype(jnp.float32)
    return (rows + branches).astype(jnp.bfloat16)
```

```python
import jax
import jax.numpy as jnp
from jax import lax
from jax.sharding import Mesh, PartitionSpec as P

HD = 128
PATCHES = 256
FSDP = ("yh", "z", "c")
MP = ("yl", "x")
ROW = ("z", "c")
SWAP = [(0, 1), (1, 0)]


def layer_norm(values, gain):
    mean = jnp.mean(values, axis=-1, keepdims=True)
    centred = values - mean
    variance = jnp.mean(centred * centred, axis=-1, keepdims=True)
    return centred * lax.rsqrt(variance + 1e-06) * gain


def shift(n, k):
    return [(i, (i + k) % n) for i in range(n)]


def gather_tokens(tokens):
    rows, cols = tokens.shape
    yl, x = lax.axis_index("yl"), lax.axis_index("x")
    other = lax.ppermute(tokens, "yl", SWAP)
    first = jnp.where(yl == 0, tokens, other)
    second = jnp.where(yl == 0, other, tokens)
    pair = jnp.stack([first, second])
    right = lax.ppermute(pair, "x", shift(4, 1))
    left = lax.ppermute(pair, "x", shift(4, -1))
    half = rows // 2
    far_a = lax.ppermute(right[:, :half], "x", shift(4, 1))
    far_b = lax.ppermute(left[:, half:], "x", shift(4, -1))
    far = jnp.concatenate([far_a, far_b], axis=1)
    by_shift = [pair, right, far, left]
    panels = []
    for h in range(2):
        for k in range(4):
            d = (x - k) % 4
            pick = by_shift[0][h]
            for s in (1, 2, 3):
                pick = jnp.where(d == s, by_shift[s][h], pick)
            panels.append(pick)
    return jnp.concatenate(panels, axis=1)


def both_rows(mine, other):
    yh = lax.axis_index("yh")
    return jnp.where(yh == 0, jnp.stack([mine, other]), jnp.stack([other, mine]))


def scatter_terms(terms):
    n = terms.shape[0] // 8
    yl, x = lax.axis_index("yl"), lax.axis_index("x")
    blocks = terms.reshape(2, 4, n, terms.shape[1])
    total = lax.dynamic_index_in_dim(blocks, x, 1, keepdims=False).astype(jnp.float32)
    for k in (1, 3, 2):
        send = lax.dynamic_index_in_dim(blocks, (x + k) % 4, 1, keepdims=False)
        total = total + lax.ppermute(send, "x", shift(4, k)).astype(jnp.float32)
    send = lax.dynamic_index_in_dim(total, 1 - yl, 0, keepdims=False).astype(jnp.bfloat16)
    got = lax.ppermute(send, "yl", SWAP).astype(jnp.float32)
    return lax.dynamic_index_in_dim(total, yl, 0, keepdims=False) + got


def local(tokens, ln_gain, w_qkv, w_up, q_gain, k_gain, w_proj, w_down):
    yh, c = lax.axis_index("yh"), lax.axis_index("c")
    tok_count = tokens.shape[0]
    head_cols = w_qkv.shape[2]
    heads_here = q_gain.shape[0]

    own_qkv = lax.all_gather(w_qkv.transpose(1, 0, 2), ROW, axis=1, tiled=True)
    quarter = own_qkv.shape[1] // 2
    up_pair = both_rows(w_up, lax.ppermute(w_up, "yh", SWAP))
    w_out = jnp.concatenate([w_proj.T, w_down.T], axis=1)
    out_pair = both_rows(w_out, lax.ppermute(w_out, "yh", SWAP))
    up_all = lax.all_gather(up_pair, ROW, axis=1, tiled=True).reshape(-1, w_up.shape[1])
    mine = lax.dynamic_slice_in_dim(own_qkv, c * quarter, quarter, axis=1)
    other_c = lax.ppermute(mine, "yh", SWAP)
    other_d = lax.ppermute(other_c, "c", SWAP)

    panels = gather_tokens(tokens)
    normed = layer_norm(panels.astype(jnp.float32), ln_gain).astype(jnp.bfloat16)

    def cols(start, size):
        return lax.dynamic_slice_in_dim(normed, start, size, axis=1)

    def dot(a, b):
        return jnp.einsum("td,cda->cta", a, b, preferred_element_type=jnp.float32)

    base = (1 - yh) * 2 * quarter
    projected = dot(cols(yh * 2 * quarter, 2 * quarter), own_qkv)
    projected = projected + dot(cols(base + c * quarter, quarter), other_c)
    projected = projected + dot(cols(base + (1 - c) * quarter, quarter), other_d)

    images = tok_count // PATCHES
    queries = layer_norm(projected[0].reshape(tok_count, heads_here, HD), q_gain).astype(
        jnp.bfloat16
    )
    keys = layer_norm(projected[1].reshape(tok_count, heads_here, HD), k_gain).astype(jnp.bfloat16)
    values = projected[2].reshape(tok_count, heads_here, HD).astype(jnp.bfloat16)
    queries = queries.reshape(images, PATCHES, heads_here, HD)
    keys = keys.reshape(images, PATCHES, heads_here, HD)
    values = values.reshape(images, PATCHES, heads_here, HD)
    scores = jnp.einsum(
        "iqhd,ikhd->ihqk", queries, keys, preferred_element_type=jnp.float32
    ) * HD ** (-0.5)
    scores = scores - jnp.max(scores, axis=-1, keepdims=True)
    weights = jnp.exp(scores)
    probs = (weights / jnp.sum(weights, axis=-1, keepdims=True)).astype(jnp.bfloat16)
    attended = jnp.einsum("ihqk,ikhd->iqhd", probs, values, preferred_element_type=jnp.float32)
    attended = attended.astype(jnp.bfloat16).reshape(tok_count, head_cols)

    hidden_pre = jnp.dot(normed, up_all, preferred_element_type=jnp.float32)
    activated = jax.nn.gelu(hidden_pre, approximate=False).astype(jnp.bfloat16)
    joined = jnp.concatenate([attended, activated], axis=1)

    parts = 2
    piece = w_out.shape[0] // parts
    sums = []
    for i in range(parts):
        part = out_pair[:, i * piece : (i + 1) * piece]
        rows = lax.all_gather(part, ROW, axis=1, tiled=True).reshape(-1, w_out.shape[1])
        terms = lax.dot_general(
            rows, joined, (((1,), (1,)), ((), ())), preferred_element_type=jnp.float32
        ).astype(jnp.bfloat16)
        sums.append(scatter_terms(terms).reshape(4, piece, tok_count))
    branches = jnp.concatenate(sums, axis=1).reshape(4 * w_out.shape[0], tok_count)
    return (tokens.astype(jnp.float32) + branches.T).astype(jnp.bfloat16)


def solution(mesh):
    fine = Mesh(mesh.devices.reshape(2, 8, 2, 2, 4), ("yh", "z", "c", "yl", "x"))
    return jax.shard_map(
        local,
        mesh=fine,
        in_specs=(
            P(FSDP, MP),
            P(),
            P(FSDP, None, MP),
            P(FSDP, MP),
            P(MP, None),
            P(MP, None),
            P(MP, FSDP),
            P(MP, FSDP),
        ),
        out_specs=P(FSDP, MP),
        check_vma=False,
    )
```

```python
import jax
import jax.numpy as jnp
from jax import lax
from jax.sharding import Mesh, PartitionSpec as P

HD = 128
PATCHES = 256
FSDP = ("yh", "z", "c")
MP = ("yl", "x")
ROW = ("z", "c")
SWAP = [(0, 1), (1, 0)]


def layer_norm(values, gain):
    mean = jnp.mean(values, axis=-1, keepdims=True)
    centred = values - mean
    variance = jnp.mean(centred * centred, axis=-1, keepdims=True)
    return centred * lax.rsqrt(variance + 1e-06) * gain


def shift(n, k):
    return [(i, (i + k) % n) for i in range(n)]


def tie(values, *after):
    return lax.optimization_barrier((values, *after))[0]


def gather_tokens(tokens, other):
    rows, cols = tokens.shape
    yl, x = lax.axis_index("yl"), lax.axis_index("x")
    first = jnp.where(yl == 0, tokens, other)
    second = jnp.where(yl == 0, other, tokens)
    pair = jnp.stack([first, second])
    right = lax.ppermute(pair, "x", shift(4, 1))
    left = lax.ppermute(pair, "x", shift(4, -1))
    half = rows // 2
    far_a = lax.ppermute(right[:, :half], "x", shift(4, 1))
    far_b = lax.ppermute(left[:, half:], "x", shift(4, -1))
    far = jnp.concatenate([far_a, far_b], axis=1)
    by_shift = [pair, right, far, left]
    panels = []
    for h in range(2):
        for k in range(4):
            d = (x - k) % 4
            pick = by_shift[0][h]
            for s in (1, 2, 3):
                pick = jnp.where(d == s, by_shift[s][h], pick)
            panels.append(pick)
    return jnp.concatenate(panels, axis=1), (right, left)


def both_rows(mine, other):
    yh = lax.axis_index("yh")
    return jnp.where(yh == 0, jnp.stack([mine, other]), jnp.stack([other, mine]))


def scatter_terms(terms):
    n = terms.shape[0] // 8
    yl, x = lax.axis_index("yl"), lax.axis_index("x")
    blocks = terms.reshape(2, 4, n, terms.shape[1])
    total = lax.dynamic_index_in_dim(blocks, x, 1, keepdims=False).astype(jnp.float32)
    for k in (1, 3, 2):
        send = lax.dynamic_index_in_dim(blocks, (x + k) % 4, 1, keepdims=False)
        total = total + lax.ppermute(send, "x", shift(4, k)).astype(jnp.float32)
    send = lax.dynamic_index_in_dim(total, 1 - yl, 0, keepdims=False).astype(jnp.bfloat16)
    got = lax.ppermute(send, "yl", SWAP).astype(jnp.float32)
    return lax.dynamic_index_in_dim(total, yl, 0, keepdims=False) + got


def ring_gather(shard, gates):
    yh, z = lax.axis_index("yh"), lax.axis_index("z")
    rows, cols = shard.shape
    held = jnp.zeros((2, 8, rows, cols), shard.dtype)

    def put(held, piece, row, offset, start=0):
        at = (row, lax.rem(z + offset + 8, 8), start, 0)
        return lax.dynamic_update_slice(held, piece[None, None], at)

    def up(v):
        return lax.ppermute(v, "z", shift(8, 1))

    def down(v):
        return lax.ppermute(v, "z", shift(8, -1))

    def across(v):
        return lax.ppermute(v, "yh", SWAP)

    held = put(held, shard, yh, 0)
    low, high = up(shard), down(shard)
    other = across(shard)
    held = put(held, other, 1 - yh, 0)
    for k in (1, 2, 3):
        low, high = tie((low, high), gates[k - 1])
        if k < 3:
            next_low, next_high = up(low), down(high)
        else:
            half = rows // 2
            next_low, next_high = up(low[:half]), down(high[half:])
        other_low, other_high = across(low), across(high)
        held = put(held, low, yh, -k)
        held = put(held, high, yh, k)
        held = put(held, other_low, 1 - yh, -k)
        held = put(held, other_high, 1 - yh, k)
        low, high = next_low, next_high
    held = put(held, low, yh, 4)
    held = put(held, high, yh, 4, half)
    held = put(held, across(low), 1 - yh, 4)
    held = put(held, across(high), 1 - yh, 4, half)
    return held.reshape(16 * rows, cols)


def local(tokens, ln_gain, w_qkv, w_up, q_gain, k_gain, w_proj, w_down):
    yh, c = lax.axis_index("yh"), lax.axis_index("c")
    tok_count = tokens.shape[0]
    head_cols = w_qkv.shape[2]
    heads_here = q_gain.shape[0]

    own_qkv = lax.all_gather(w_qkv.transpose(1, 0, 2), ROW, axis=1, tiled=True)
    quarter = own_qkv.shape[1] // 2
    other_up, other_tokens = lax.optimization_barrier(
        (lax.ppermute(w_up, "yh", SWAP), lax.ppermute(tokens, "yl", SWAP))
    )
    up_pair = both_rows(w_up, other_up)
    up_all = lax.all_gather(up_pair, ROW, axis=1, tiled=True).reshape(-1, w_up.shape[1])
    mine = lax.dynamic_slice_in_dim(own_qkv, c * quarter, quarter, axis=1)
    other_c = lax.ppermute(mine, "yh", SWAP)
    other_d = lax.ppermute(other_c, "c", SWAP)

    panels, near = gather_tokens(tokens, other_tokens)
    normed = layer_norm(panels.astype(jnp.float32), ln_gain).astype(jnp.bfloat16)
    w_out = jnp.concatenate([w_proj.T, w_down.T], axis=1)
    w_out = tie(w_out, other_tokens)
    out_rows = ring_gather(w_out, (near, mine, mine))

    def cols(start, size):
        return lax.dynamic_slice_in_dim(normed, start, size, axis=1)

    def dot(a, b):
        return jnp.einsum("td,cda->cta", a, b, preferred_element_type=jnp.float32)

    base = (1 - yh) * 2 * quarter
    projected = dot(cols(yh * 2 * quarter, 2 * quarter), own_qkv)
    projected = projected + dot(cols(base + c * quarter, quarter), other_c)
    projected = projected + dot(cols(base + (1 - c) * quarter, quarter), other_d)

    images = tok_count // PATCHES
    queries = layer_norm(projected[0].reshape(tok_count, heads_here, HD), q_gain).astype(
        jnp.bfloat16
    )
    keys = layer_norm(projected[1].reshape(tok_count, heads_here, HD), k_gain).astype(jnp.bfloat16)
    values = projected[2].reshape(tok_count, heads_here, HD).astype(jnp.bfloat16)
    queries = queries.reshape(images, PATCHES, heads_here, HD)
    keys = keys.reshape(images, PATCHES, heads_here, HD)
    values = values.reshape(images, PATCHES, heads_here, HD)
    scores = jnp.einsum(
        "iqhd,ikhd->ihqk", queries, keys, preferred_element_type=jnp.float32
    ) * HD ** (-0.5)
    scores = scores - jnp.max(scores, axis=-1, keepdims=True)
    weights = jnp.exp(scores)
    probs = (weights / jnp.sum(weights, axis=-1, keepdims=True)).astype(jnp.bfloat16)
    attended = jnp.einsum("ihqk,ikhd->iqhd", probs, values, preferred_element_type=jnp.float32)
    attended = attended.astype(jnp.bfloat16).reshape(tok_count, head_cols)

    hidden_pre = jnp.dot(tie(normed, attended), up_all, preferred_element_type=jnp.float32)
    activated = jax.nn.gelu(hidden_pre, approximate=False).astype(jnp.bfloat16)

    def branch_sums(attended, activated):
        joined = jnp.concatenate([attended, activated], axis=1)
        terms = lax.dot_general(
            out_rows, joined, (((1,), (1,)), ((), ())), preferred_element_type=jnp.float32
        ).astype(jnp.bfloat16)
        return scatter_terms(terms)

    sibling = branch_sums(
        lax.ppermute(attended, "c", SWAP), lax.ppermute(activated, "c", SWAP)
    )
    mine = branch_sums(attended, activated)
    theirs = lax.ppermute(sibling, "c", SWAP)
    piece = w_out.shape[0]
    mine = mine.reshape(2, 1, piece, tok_count)
    theirs = theirs.reshape(2, 1, piece, tok_count)
    even = jnp.where(c == 0, mine, theirs)
    odd = jnp.where(c == 0, theirs, mine)
    branches = jnp.concatenate([even, odd], axis=1).reshape(4 * piece, tok_count)
    return (tokens.astype(jnp.float32) + branches.T).astype(jnp.bfloat16)


def solution(mesh):
    fine = Mesh(mesh.devices.reshape(2, 8, 2, 2, 4), ("yh", "z", "c", "yl", "x"))
    return jax.shard_map(
        local,
        mesh=fine,
        in_specs=(
            P(FSDP, MP),
            P(),
            P(FSDP, None, MP),
            P(FSDP, MP),
            P(MP, None),
            P(MP, None),
            P(MP, FSDP),
            P(MP, FSDP),
        ),
        out_specs=P(FSDP, MP),
        check_vma=False,
    )
```

```python
import jax
import jax.numpy as jnp
from jax import lax
from jax.experimental import pallas as pl
from jax.experimental.pallas import tpu as pltpu
from jax.sharding import Mesh, PartitionSpec as P

HD = 128
PATCHES = 256
FSDP = ("yh", "z", "c")
MP = ("yl", "x")
ROW = ("z", "c")
SWAP = [(0, 1), (1, 0)]


def layer_norm(values, gain):
    mean = jnp.mean(values, axis=-1, keepdims=True)
    centred = values - mean
    variance = jnp.mean(centred * centred, axis=-1, keepdims=True)
    return centred * lax.rsqrt(variance + 1e-06) * gain


def shift(n, k):
    return [(i, (i + k) % n) for i in range(n)]


def tie(values, *after):
    return lax.optimization_barrier((values, *after))[0]


def gather_tokens(tokens, other):
    rows, cols = tokens.shape
    yl, x = lax.axis_index("yl"), lax.axis_index("x")
    first = jnp.where(yl == 0, tokens, other)
    second = jnp.where(yl == 0, other, tokens)
    pair = jnp.stack([first, second])
    right = lax.ppermute(pair, "x", shift(4, 1))
    left = lax.ppermute(pair, "x", shift(4, -1))
    half = rows // 2
    far_a = lax.ppermute(right[:, :half], "x", shift(4, 1))
    far_b = lax.ppermute(left[:, half:], "x", shift(4, -1))
    far = jnp.concatenate([far_a, far_b], axis=1)
    by_shift = [pair, right, far, left]
    panels = []
    for h in range(2):
        for k in range(4):
            d = (x - k) % 4
            pick = by_shift[0][h]
            for s in (1, 2, 3):
                pick = jnp.where(d == s, by_shift[s][h], pick)
            panels.append(pick)
    return jnp.concatenate(panels, axis=1)


def both_rows(mine, other):
    yh = lax.axis_index("yh")
    return jnp.where(yh == 0, jnp.stack([mine, other]), jnp.stack([other, mine]))


def scatter_sends(terms, hop):
    n = terms.shape[0] // 8
    x = lax.axis_index("x")
    blocks = terms.reshape(2, 4, n, terms.shape[1])
    arrived = []
    for k in (2, 1, 3, 0):
        block = lax.dynamic_index_in_dim(blocks, (x + k) % 4, 1, keepdims=False)
        if k or hop:
            perm = [
                (core * 4 + at, (core ^ hop) * 4 + (at + k) % 4) for core in range(2) for at in range(4)
            ]
            block = lax.ppermute(block, ("c", "x"), perm)
        arrived.append(block)
    return arrived


def scatter_sum(arrived):
    yl = lax.axis_index("yl")
    total = sum(v.astype(jnp.float32) for v in arrived)
    send = lax.dynamic_index_in_dim(total, 1 - yl, 0, keepdims=False).astype(jnp.bfloat16)
    other = lax.ppermute(send, "yl", SWAP).astype(jnp.float32)
    return lax.dynamic_index_in_dim(total, yl, 0, keepdims=False) + other


def across(v):
    return lax.ppermute(v, "yh", SWAP)


def ring_z(shard):
    half = shard.shape[0] // 2

    def up(v):
        return lax.ppermute(v, "z", shift(8, 1))

    def down(v):
        return lax.ppermute(v, "z", shift(8, -1))

    held = {0: [(0, shard)], -1: [(0, up(shard))], 1: [(0, down(shard))]}
    for k in (2, 3):
        held[-k] = [(0, up(held[1 - k][0][1]))]
        held[k] = [(0, down(held[k - 1][0][1]))]
    held[4] = [(0, up(held[-3][0][1][:half])), (half, down(held[3][0][1][half:]))]
    return held


def up_kernel(x_ref, w_ref, out_ref):
    pre = jnp.dot(x_ref[...], w_ref[...], preferred_element_type=jnp.float32)
    out_ref[...] = (0.5 * pre * (1.0 + lax.erf(pre * 0.7071067811865476))).astype(out_ref.dtype)


def up_gelu(x, w):
    tile = 256
    rows, depth = x.shape
    hidden = w.shape[1]
    return pl.pallas_call(
        up_kernel,
        grid=(hidden // tile,),
        in_specs=[
            pl.BlockSpec((rows, depth), lambda i: (0, 0)),
            pl.BlockSpec((depth, tile), lambda i: (0, i)),
        ],
        out_specs=pl.BlockSpec((rows, tile), lambda i: (0, i)),
        out_shape=jax.ShapeDtypeStruct((rows, hidden), jnp.bfloat16),
        compiler_params=pltpu.CompilerParams(vmem_limit_bytes=40 * 2**20),
        cost_estimate=pl.CostEstimate(
            flops=2 * rows * depth * hidden,
            bytes_accessed=2 * (rows * depth + depth * hidden + rows * hidden),
            transcendentals=rows * hidden,
        ),
    )(x, w)


def local(tokens, ln_gain, w_qkv, w_up, q_gain, k_gain, w_proj, w_down):
    yh, z, c = lax.axis_index("yh"), lax.axis_index("z"), lax.axis_index("c")
    tok_count = tokens.shape[0]
    head_cols = w_qkv.shape[2]
    heads_here = q_gain.shape[0]

    own_qkv = lax.all_gather(w_qkv.transpose(1, 0, 2), ROW, axis=1, tiled=True)
    quarter = own_qkv.shape[1] // 2
    other_up, other_tokens = lax.optimization_barrier(
        (lax.ppermute(w_up, "yh", SWAP), lax.ppermute(tokens, "yl", SWAP))
    )
    up_pair = both_rows(w_up, other_up)
    up_all = lax.all_gather(up_pair, ROW, axis=1, tiled=True).reshape(-1, w_up.shape[1])
    mine = lax.dynamic_slice_in_dim(own_qkv, c * quarter, quarter, axis=1)
    other_c = lax.ppermute(mine, "yh", SWAP)
    other_d = lax.ppermute(other_c, "c", SWAP)

    panels = gather_tokens(tokens, other_tokens)
    normed = layer_norm(panels.astype(jnp.float32), ln_gain).astype(jnp.bfloat16)
    w_out = jnp.concatenate([w_proj.T, w_down.T], axis=1)
    w_out = tie(w_out, other_tokens)
    piece = w_out.shape[0]
    out_rows = jnp.zeros((2, 8, piece, w_out.shape[1]), w_out.dtype)

    def put(out_rows, row, offset, pieces):
        for start, values in pieces:
            at = (row, lax.rem(z + offset + 8, 8), start, 0)
            out_rows = lax.dynamic_update_slice(out_rows, values[None, None], at)
        return out_rows

    own = ring_z(w_out)
    for k, pieces in own.items():
        out_rows = put(out_rows, yh, k, pieces)
    for k in (0, -1, 1):
        out_rows = put(out_rows, 1 - yh, k, [(0, across(own[k][0][1]))])

    def crossing(offsets, gate):
        pieces = tie([own[k] for k in offsets], gate)
        return {k: [(at, across(v)) for at, v in piece] for k, piece in zip(offsets, pieces)}

    far = crossing((-2, 2), other_d)
    def cols(start, size):
        return lax.dynamic_slice_in_dim(normed, start, size, axis=1)

    def dot(a, b):
        return jnp.einsum("td,cda->cta", a, b, preferred_element_type=jnp.float32)

    base = (1 - yh) * 2 * quarter
    projected = dot(cols(yh * 2 * quarter, 2 * quarter), own_qkv)
    projected = projected + dot(cols(base + c * quarter, quarter), other_c)
    projected = projected + dot(cols(base + (1 - c) * quarter, quarter), other_d)

    far |= crossing((-3, 3), projected)

    images = tok_count // PATCHES
    queries = layer_norm(projected[0].reshape(tok_count, heads_here, HD), q_gain).astype(
        jnp.bfloat16
    )
    keys = layer_norm(projected[1].reshape(tok_count, heads_here, HD), k_gain).astype(jnp.bfloat16)
    values = projected[2].reshape(tok_count, heads_here, HD).astype(jnp.bfloat16)
    queries = queries.reshape(images, PATCHES, heads_here, HD)
    keys = keys.reshape(images, PATCHES, heads_here, HD)
    values = values.reshape(images, PATCHES, heads_here, HD)
    scores = jnp.einsum(
        "iqhd,ikhd->ihqk", queries, keys, preferred_element_type=jnp.float32
    ) * HD ** (-0.5)
    scores = scores - jnp.max(scores, axis=-1, keepdims=True)
    weights = jnp.exp(scores)
    probs = (weights / jnp.sum(weights, axis=-1, keepdims=True)).astype(jnp.bfloat16)
    attended = jnp.einsum("ihqk,ikhd->iqhd", probs, values, preferred_element_type=jnp.float32)
    attended = attended.astype(jnp.bfloat16).reshape(tok_count, head_cols)

    last = crossing((4,), attended)
    far = tie(far, attended)
    for k in far:
        out_rows = put(out_rows, 1 - yh, k, far[k])
    normed, out_rows = lax.optimization_barrier((normed, out_rows))
    activated = up_gelu(normed, up_all)
    last = tie(last, activated)
    out_rows = put(out_rows, 1 - yh, 4, last[4]).reshape(16 * piece, -1)

    def terms_of(attended, activated):
        joined = jnp.concatenate([attended, activated], axis=1)
        return lax.dot_general(
            out_rows, joined, (((1,), (1,)), ((), ())), preferred_element_type=jnp.float32
        ).astype(jnp.bfloat16)

    mine = scatter_sends(terms_of(attended, activated), 0)
    theirs = scatter_sends(
        terms_of(lax.ppermute(attended, "c", SWAP), lax.ppermute(activated, "c", SWAP)), 1
    )
    mine = tie(mine, theirs[0])
    mine, theirs = scatter_sum(mine), scatter_sum(theirs)
    mine = mine.reshape(2, 1, piece, tok_count)
    theirs = theirs.reshape(2, 1, piece, tok_count)
    even = jnp.where(c == 0, mine, theirs)
    odd = jnp.where(c == 0, theirs, mine)
    branches = jnp.concatenate([even, odd], axis=1).reshape(4 * piece, tok_count)
    return (tokens.astype(jnp.float32) + branches.T).astype(jnp.bfloat16)


def solution(mesh):
    fine = Mesh(mesh.devices.reshape(2, 8, 2, 2, 4), ("yh", "z", "c", "yl", "x"))
    return jax.shard_map(
        local,
        mesh=fine,
        in_specs=(
            P(FSDP, MP),
            P(),
            P(FSDP, None, MP),
            P(FSDP, MP),
            P(MP, None),
            P(MP, None),
            P(MP, FSDP),
            P(MP, FSDP),
        ),
        out_specs=P(FSDP, MP),
        check_vma=False,
    )
```

```python
import functools

import jax
import jax.numpy as jnp
from jax import lax
from jax.experimental import pallas as pl
from jax.experimental.pallas import tpu as pltpu
from jax.sharding import Mesh, PartitionSpec as P

HD = 128
PATCHES = 256
FSDP = ("yh", "z", "c")
MP = ("yl", "x")
ROW = ("z", "c")
SWAP = [(0, 1), (1, 0)]


def layer_norm(values, gain):
    mean = jnp.mean(values, axis=-1, keepdims=True)
    centred = values - mean
    variance = jnp.mean(centred * centred, axis=-1, keepdims=True)
    return centred * lax.rsqrt(variance + 1e-06) * gain


def shift(n, k):
    return [(i, (i + k) % n) for i in range(n)]


def tie(values, *after):
    return lax.optimization_barrier((values, *after))[0]


def place_tokens(by_shift):
    x = lax.axis_index("x")
    panels = []
    for h in range(2):
        for k in range(4):
            d = (x - k) % 4
            pick = by_shift[0][h]
            for s in (1, 2, 3):
                pick = jnp.where(d == s, by_shift[s][h], pick)
            panels.append(pick)
    return jnp.concatenate(panels, axis=1)


def both_rows(mine, other):
    yh = lax.axis_index("yh")
    return jnp.where(yh == 0, jnp.stack([mine, other]), jnp.stack([other, mine]))


def scatter_sends(terms, hop):
    n = terms.shape[0] // 8
    x = lax.axis_index("x")
    blocks = terms.reshape(2, 4, n, terms.shape[1])
    arrived = []
    for k in (2, 1, 3, 0):
        block = lax.dynamic_index_in_dim(blocks, (x + k) % 4, 1, keepdims=False)
        if k or hop:
            perm = [
                (core * 4 + at, (core ^ hop) * 4 + (at + k) % 4) for core in range(2) for at in range(4)
            ]
            block = lax.ppermute(block, ("c", "x"), perm)
        arrived.append(block)
    return arrived


def scatter_sum(arrived):
    yl = lax.axis_index("yl")
    total = sum(v.astype(jnp.float32) for v in arrived)
    send = lax.dynamic_index_in_dim(total, 1 - yl, 0, keepdims=False).astype(jnp.bfloat16)
    other = lax.ppermute(send, "yl", SWAP).astype(jnp.float32)
    return lax.dynamic_index_in_dim(total, yl, 0, keepdims=False) + other


def across(v):
    return lax.ppermute(v, "yh", SWAP)


def up_kernel(x_ref, w_ref, out_ref):
    pre = jnp.dot(x_ref[...], w_ref[...], preferred_element_type=jnp.float32)
    out_ref[...] = (0.5 * pre * (1.0 + lax.erf(pre * 0.7071067811865476))).astype(out_ref.dtype)


def up_gelu(x, w):
    tile = 256
    rows, depth = x.shape
    hidden = w.shape[1]
    return pl.pallas_call(
        up_kernel,
        grid=(hidden // tile,),
        in_specs=[
            pl.BlockSpec((rows, depth), lambda i: (0, 0)),
            pl.BlockSpec((depth, tile), lambda i: (0, i)),
        ],
        out_specs=pl.BlockSpec((rows, tile), lambda i: (0, i)),
        out_shape=jax.ShapeDtypeStruct((rows, hidden), jnp.bfloat16),
        compiler_params=pltpu.CompilerParams(vmem_limit_bytes=40 * 2**20),
        cost_estimate=pl.CostEstimate(
            flops=2 * rows * depth * hidden,
            bytes_accessed=2 * (rows * depth + depth * hidden + rows * hidden),
            transcendentals=rows * hidden,
        ),
    )(x, w)


def attention_kernel(
    starts_ref, x_ref, own_ref, near_ref, far_ref, q_gain_ref, k_gain_ref, out_ref, proj_ref
):
    rows, heads = x_ref.shape[0], q_gain_ref.shape[0]
    pieces = (own_ref, near_ref, far_ref)
    for part in range(3):
        total = None
        for i, w_ref in enumerate(pieces):
            depth = w_ref.shape[1]
            at = pl.multiple_of(starts_ref[i], HD)
            term = jnp.dot(
                x_ref[:, pl.ds(at, depth)], w_ref[part], preferred_element_type=jnp.float32
            )
            total = term if total is None else total + term
        proj_ref[part] = total
    for h in range(heads):
        cols = slice(h * HD, (h + 1) * HD)
        q_gain, k_gain = q_gain_ref[h : h + 1, :], k_gain_ref[h : h + 1, :]
        for image in range(rows // PATCHES):
            at = slice(image * PATCHES, (image + 1) * PATCHES)
            queries = layer_norm(proj_ref[0, at, cols], q_gain).astype(jnp.bfloat16)
            keys = layer_norm(proj_ref[1, at, cols], k_gain).astype(jnp.bfloat16)
            values = proj_ref[2, at, cols].astype(jnp.bfloat16)
            scores = lax.dot_general(
                queries, keys, (((1,), (1,)), ((), ())), preferred_element_type=jnp.float32
            ) * HD ** (-0.5)
            scores = scores - jnp.max(scores, axis=-1, keepdims=True)
            weights = jnp.exp(scores)
            probs = (weights / jnp.sum(weights, axis=-1, keepdims=True)).astype(jnp.bfloat16)
            mixed = jnp.dot(probs, values, preferred_element_type=jnp.float32)
            out_ref[at, cols] = mixed.astype(jnp.bfloat16)


def attention(starts, x, own, near, far, q_gain, k_gain):
    rows, depth = x.shape
    cols = own.shape[2]
    vmem = pl.BlockSpec(memory_space=pltpu.VMEM)
    return pl.pallas_call(
        attention_kernel,
        in_specs=[pl.BlockSpec(memory_space=pltpu.SMEM)] + [vmem] * 6,
        out_specs=vmem,
        out_shape=jax.ShapeDtypeStruct((rows, cols), jnp.bfloat16),
        scratch_shapes=[pltpu.VMEM((3, rows, cols), jnp.float32)],
        compiler_params=pltpu.CompilerParams(vmem_limit_bytes=40 * 2**20),
        cost_estimate=pl.CostEstimate(
            flops=6 * rows * depth * cols,
            bytes_accessed=6 * depth * cols + 2 * rows * depth,
            transcendentals=rows * PATCHES * cols // HD,
        ),
    )(starts, x, own, near, far, q_gain, k_gain)


def out_kernel(places, rows, *refs):
    at_ref, attended_ref, activated_ref = refs[:3]
    shards = refs[3 : 3 + len(places)]
    out_ref, held, sem = refs[3 + len(places) :]
    yh, z = at_ref[0], at_ref[1]
    copies = []
    for i, ((other, offset, start), shard) in enumerate(zip(places, shards)):
        row = 1 - yh if other else yh
        at = (row * 8 + lax.rem(z + offset + 8, 8)) * rows + start
        at = pl.multiple_of(at, 16)
        copy = pltpu.make_async_copy(shard, held.at[pl.ds(at, shard.shape[0])], sem.at[i])
        copy.start()
        copies.append(copy)
    for copy in copies:
        copy.wait()
    split = attended_ref.shape[1]
    block = 4 * rows
    contract = (((1,), (1,)), ((), ()))

    @pl.loop(0, held.shape[0] // block)
    def _(i):
        at = pl.ds(pl.multiple_of(i * block, 16), block)
        total = lax.dot_general(
            held[at, :split], attended_ref[...], contract, preferred_element_type=jnp.float32
        )
        total += lax.dot_general(
            held[at, split:], activated_ref[...], contract, preferred_element_type=jnp.float32
        )
        out_ref[at, :] = total.astype(out_ref.dtype)


def out_terms(place, rows, attended, activated, shards):
    places = tuple(shards)
    tokens = attended.shape[0]
    width = attended.shape[1] + activated.shape[1]
    vmem = pl.BlockSpec(memory_space=pltpu.VMEM)
    return pl.pallas_call(
        functools.partial(out_kernel, places, rows),
        in_specs=[pl.BlockSpec(memory_space=pltpu.SMEM), vmem, vmem]
        + [pl.BlockSpec(memory_space=pl.ANY)] * len(places),
        out_specs=vmem,
        out_shape=jax.ShapeDtypeStruct((16 * rows, tokens), jnp.bfloat16),
        scratch_shapes=[
            pltpu.VMEM((16 * rows, width), jnp.bfloat16),
            pltpu.SemaphoreType.DMA((len(places),)),
        ],
        compiler_params=pltpu.CompilerParams(vmem_limit_bytes=40 * 2**20),
        cost_estimate=pl.CostEstimate(
            flops=32 * rows * width * tokens,
            bytes_accessed=32 * rows * width + 2 * tokens * width + 32 * rows * tokens,
            transcendentals=0,
        ),
    )(place, attended, activated, *shards.values())


def local(tokens, ln_gain, w_qkv, w_up, q_gain, k_gain, w_proj, w_down):
    yh, z, c = lax.axis_index("yh"), lax.axis_index("z"), lax.axis_index("c")
    yl = lax.axis_index("yl")
    tok_count = tokens.shape[0]

    def up(v, axis="z", size=8):
        return lax.ppermute(v, axis, shift(size, 1))

    def down(v, axis="z", size=8):
        return lax.ppermute(v, axis, shift(size, -1))

    own_qkv = lax.all_gather(w_qkv.transpose(1, 0, 2), ROW, axis=1, tiled=True)

    w_out = jnp.concatenate([w_proj.T, w_down.T], axis=1)
    piece = w_out.shape[0]
    half = piece // 2
    other_tokens, other_up, low, high = lax.optimization_barrier(
        (lax.ppermute(tokens, "yl", SWAP), across(w_up), up(w_out), down(w_out))
    )
    up_pair = both_rows(w_up, other_up)
    up_all = lax.all_gather(up_pair, ROW, axis=1, tiled=True).reshape(-1, w_up.shape[1])
    shards = {(0, 0, 0): w_out, (0, -1, 0): low, (0, 1, 0): high}

    first = jnp.where(yl == 0, tokens, other_tokens)
    second = jnp.where(yl == 0, other_tokens, tokens)
    pair = jnp.stack([first, second])
    shards[1, 0, 0] = across(tie(w_out, other_up))
    shards[1, -1, 0], shards[1, 1, 0] = across(low), across(high)
    right, left, low, high = lax.optimization_barrier(
        (up(pair, "x", 4), down(pair, "x", 4), up(low), down(high))
    )
    shards[0, -2, 0], shards[0, 2, 0] = low, high

    middle = tok_count // 2
    far_a, far_b = up(right[:, :middle], "x", 4), down(left[:, middle:], "x", 4)
    low, high = up(low), down(high)
    shards[0, -3, 0], shards[0, 3, 0] = low, high

    quarter = own_qkv.shape[1] // 2
    mine = lax.dynamic_slice_in_dim(own_qkv, c * quarter, quarter, axis=1)
    other_c = across(mine)
    other_d = lax.ppermute(other_c, "c", SWAP)
    crossed = [shards[1, k, 0] for k in (0, -1, 1)]
    far_a, far_b, low, high = tie((far_a, far_b, low, high), mine, crossed)
    shards[0, 4, 0], shards[0, 4, half] = up(low[:half]), down(high[half:])

    far = jnp.concatenate([far_a, far_b], axis=1)
    panels = place_tokens([pair, right, far, left])
    normed = layer_norm(panels.astype(jnp.float32), ln_gain).astype(jnp.bfloat16)

    crossing = [(-2, 0), (2, 0), (-3, 0), (3, 0), (4, 0), (4, half)]
    for (k, at), v in zip(crossing, tie([shards[0, k, at] for k, at in crossing], other_d)):
        shards[1, k, at] = across(v)

    base = (1 - yh) * 2 * quarter
    starts = jnp.stack([yh * 2 * quarter, base + c * quarter, base + (1 - c) * quarter])
    normed = tie(normed, [shards[0, 4, at] for at in (0, half)])
    attended = attention(starts, normed, own_qkv, other_c, other_d, q_gain, k_gain)
    crossed = [shards[1, k, 0] for k in (-2, 2, -3, 3)]
    activated = up_gelu(tie(normed, attended, crossed), up_all)

    place = jnp.stack([yh, z])
    mine = scatter_sends(out_terms(place, piece, attended, activated, shards), 0)
    swapped = (lax.ppermute(attended, "c", SWAP), lax.ppermute(activated, "c", SWAP))
    theirs = scatter_sends(out_terms(place, piece, *swapped, shards), 1)
    mine = tie(mine, theirs[0])
    mine, theirs = scatter_sum(mine), scatter_sum(theirs)
    mine = mine.reshape(2, 1, piece, tok_count)
    theirs = theirs.reshape(2, 1, piece, tok_count)
    even = jnp.where(c == 0, mine, theirs)
    odd = jnp.where(c == 0, theirs, mine)
    branches = jnp.concatenate([even, odd], axis=1).reshape(4 * piece, tok_count)
    return (tokens.astype(jnp.float32) + branches.T).astype(jnp.bfloat16)


def solution(mesh):
    fine = Mesh(mesh.devices.reshape(2, 8, 2, 2, 4), ("yh", "z", "c", "yl", "x"))
    return jax.shard_map(
        local,
        mesh=fine,
        in_specs=(
            P(FSDP, MP),
            P(),
            P(FSDP, None, MP),
            P(FSDP, MP),
            P(MP, None),
            P(MP, None),
            P(MP, FSDP),
            P(MP, FSDP),
        ),
        out_specs=P(FSDP, MP),
        check_vma=False,
    )
```

```python
import functools

import jax
import jax.numpy as jnp
from jax import lax
from jax.experimental import pallas as pl
from jax.experimental.pallas import tpu as pltpu
from jax.sharding import Mesh, PartitionSpec as P

HD = 128
PATCHES = 256
FSDP = ("yh", "z", "c")
MP = ("yl", "x")
ROW = ("z", "c")
SWAP = [(0, 1), (1, 0)]


def layer_norm(values, gain):
    mean = jnp.mean(values, axis=-1, keepdims=True)
    centred = values - mean
    variance = jnp.mean(centred * centred, axis=-1, keepdims=True)
    return centred * lax.rsqrt(variance + 1e-06) * gain


def shift(n, k):
    return [(i, (i + k) % n) for i in range(n)]


def tie(values, *after):
    return lax.optimization_barrier((values, *after))[0]


def place_tokens(by_shift):
    x = lax.axis_index("x")
    panels = []
    for h in range(2):
        for k in range(4):
            d = (x - k) % 4
            panel = by_shift[0][h]
            for s in (1, 2, 3):
                panel = jnp.where(d == s, by_shift[s][h], panel)
            panels.append(panel)
    return jnp.concatenate(panels, axis=1)


def both_rows(mine, other):
    yh = lax.axis_index("yh")
    return jnp.where(yh == 0, jnp.stack([mine, other]), jnp.stack([other, mine]))


def pick(blocks, at, axis):
    return lax.dynamic_index_in_dim(blocks, at, axis, keepdims=False)


def to_peers_x(blocks, axis):
    x = lax.axis_index("x")
    return [
        lax.ppermute(pick(blocks, (x + k) % 4, axis), "x", shift(4, k)) for k in (2, 1, 3)
    ]


def scatter_start(mine, theirs):
    yl, x = lax.axis_index("yl"), lax.axis_index("x")
    shape = (2, 4, mine.shape[0] // 8 * mine.shape[1], mine.shape[2])
    mine, theirs = mine.reshape(shape), theirs.reshape(shape)
    over_x = to_peers_x(mine, 1)
    both = [(core * 2 + at, (1 - core) * 2 + 1 - at) for core in range(2) for at in range(2)]
    over_y = lax.ppermute(pick(theirs, 1 - yl, 0), ("c", "yl"), both)
    kept = lax.ppermute(pick(theirs, yl, 0), "c", SWAP)
    over_x = tie(over_x, kept)
    return [pick(mine, x, 1)] + over_x, [kept, over_y]


def scatter_end(over_x, over_y):
    yl, x = lax.axis_index("yl"), lax.axis_index("x")

    def total(values):
        return sum(v.astype(jnp.float32) for v in values)

    by_y, by_x = total(over_x), total(over_y)
    other = lax.ppermute(pick(by_y, 1 - yl, 0).astype(jnp.bfloat16), "yl", SWAP)
    others = to_peers_x(by_x.astype(jnp.bfloat16), 0)
    return total([pick(by_y, yl, 0), other]), total([pick(by_x, x, 0)] + others)


def across(v):
    return lax.ppermute(v, "yh", SWAP)


def up_kernel(x_ref, w_ref, out_ref):
    pre = jnp.dot(x_ref[...], w_ref[...], preferred_element_type=jnp.float32)
    out_ref[...] = (0.5 * pre * (1.0 + lax.erf(pre * 0.7071067811865476))).astype(out_ref.dtype)


def up_gelu(x, w):
    tile = 256
    rows, depth = x.shape
    hidden = w.shape[1]
    return pl.pallas_call(
        up_kernel,
        grid=(hidden // tile,),
        in_specs=[
            pl.BlockSpec((rows, depth), lambda i: (0, 0)),
            pl.BlockSpec((depth, tile), lambda i: (0, i)),
        ],
        out_specs=pl.BlockSpec((rows, tile), lambda i: (0, i)),
        out_shape=jax.ShapeDtypeStruct((rows, hidden), jnp.bfloat16),
        compiler_params=pltpu.CompilerParams(vmem_limit_bytes=58 * 2**20),
        cost_estimate=pl.CostEstimate(
            flops=2 * rows * depth * hidden,
            bytes_accessed=2 * (rows * depth + depth * hidden + rows * hidden),
            transcendentals=rows * hidden,
        ),
    )(x, w)


def attention_kernel(
    starts_ref, x_ref, own_ref, near_ref, far_ref, q_gain_ref, k_gain_ref, out_ref, proj_ref
):
    rows, heads = x_ref.shape[0], q_gain_ref.shape[0]
    pieces = (own_ref, near_ref, far_ref)
    for part in range(3):
        total = None
        for i, w_ref in enumerate(pieces):
            depth = w_ref.shape[1]
            at = pl.multiple_of(starts_ref[i], HD)
            term = jnp.dot(
                x_ref[:, pl.ds(at, depth)], w_ref[part], preferred_element_type=jnp.float32
            )
            total = term if total is None else total + term
        proj_ref[part] = total
    for h in range(heads):
        cols = slice(h * HD, (h + 1) * HD)
        q_gain, k_gain = q_gain_ref[h : h + 1, :], k_gain_ref[h : h + 1, :]
        for image in range(rows // PATCHES):
            at = slice(image * PATCHES, (image + 1) * PATCHES)
            queries = layer_norm(proj_ref[0, at, cols], q_gain).astype(jnp.bfloat16)
            keys = layer_norm(proj_ref[1, at, cols], k_gain).astype(jnp.bfloat16)
            values = proj_ref[2, at, cols].astype(jnp.bfloat16)
            scores = lax.dot_general(
                queries, keys, (((1,), (1,)), ((), ())), preferred_element_type=jnp.float32
            ) * HD ** (-0.5)
            scores = scores - jnp.max(scores, axis=-1, keepdims=True)
            weights = jnp.exp(scores)
            probs = (weights / jnp.sum(weights, axis=-1, keepdims=True)).astype(jnp.bfloat16)
            mixed = jnp.dot(probs, values, preferred_element_type=jnp.float32)
            out_ref[at, cols] = mixed.astype(jnp.bfloat16)


def attention(starts, x, own, near, far, q_gain, k_gain):
    rows, depth = x.shape
    cols = own.shape[2]
    vmem = pl.BlockSpec(memory_space=pltpu.VMEM)
    return pl.pallas_call(
        attention_kernel,
        in_specs=[pl.BlockSpec(memory_space=pltpu.SMEM)] + [vmem] * 6,
        out_specs=vmem,
        out_shape=jax.ShapeDtypeStruct((rows, cols), jnp.bfloat16),
        scratch_shapes=[pltpu.VMEM((3, rows, cols), jnp.float32)],
        compiler_params=pltpu.CompilerParams(vmem_limit_bytes=40 * 2**20),
        cost_estimate=pl.CostEstimate(
            flops=6 * rows * depth * cols,
            bytes_accessed=6 * depth * cols + 2 * rows * depth,
            transcendentals=rows * PATCHES * cols // HD,
        ),
    )(starts, x, own, near, far, q_gain, k_gain)


def out_kernel(places, rows, *refs):
    at_ref, attended_ref, activated_ref = refs[:3]
    shards = refs[3 : 3 + len(places)]
    out_ref, held, sem = refs[3 + len(places) :]
    yh, z = at_ref[0], at_ref[1]
    slots = list(dict.fromkeys(place[:2] for group in places for place in group))
    copies = [[] for _ in slots]
    count = 0
    for group, shard in zip(places, shards):
        for i, (other, offset, start) in enumerate(group):
            slot = slots.index((other, offset))
            at = pl.ds(slot * rows + start, shard.shape[1])
            copy = pltpu.make_async_copy(shard.at[i], held.at[at], sem.at[count])
            copy.start()
            copies[slot].append(copy)
            count += 1
    split = attended_ref.shape[1]
    contract = (((1,), (1,)), ((), ()))
    step = 4
    for first in range(0, len(slots), step):
        for slot in range(first, first + step):
            for copy in copies[slot]:
                copy.wait()
        at = slice(first * rows, (first + step) * rows)
        total = lax.dot_general(
            held[at, :split], attended_ref[...], contract, preferred_element_type=jnp.float32
        )
        total += lax.dot_general(
            held[at, split:], activated_ref[...], contract, preferred_element_type=jnp.float32
        )
        total = total.astype(out_ref.dtype)
        for i in range(step):
            other, offset = slots[first + i]
            owner = (1 - yh if other else yh) * 8 + lax.rem(z + offset + 8, 8)
            out_ref[owner] = total[i * rows : (i + 1) * rows]


def out_terms(place, rows, attended, activated, shards):
    places = tuple(places for places, _ in shards)
    tokens = attended.shape[0]
    width = attended.shape[1] + activated.shape[1]
    vmem = pl.BlockSpec(memory_space=pltpu.VMEM)
    return pl.pallas_call(
        functools.partial(out_kernel, places, rows),
        in_specs=[pl.BlockSpec(memory_space=pltpu.SMEM), vmem, vmem]
        + [pl.BlockSpec(memory_space=pltpu.HBM)] * len(places),
        out_specs=vmem,
        out_shape=jax.ShapeDtypeStruct((16, rows, tokens), jnp.bfloat16),
        scratch_shapes=[
            pltpu.VMEM((16 * rows, width), jnp.bfloat16),
            pltpu.SemaphoreType.DMA((sum(len(group) for group in places),)),
        ],
        compiler_params=pltpu.CompilerParams(vmem_limit_bytes=40 * 2**20),
        cost_estimate=pl.CostEstimate(
            flops=32 * rows * width * tokens,
            bytes_accessed=32 * rows * width + 2 * tokens * width + 32 * rows * tokens,
            transcendentals=0,
        ),
    )(place, attended, activated, *(arrays for _, arrays in shards))


def local(tokens, ln_gain, w_qkv, w_up, q_gain, k_gain, w_proj, w_down):
    yh, z, c = lax.axis_index("yh"), lax.axis_index("z"), lax.axis_index("c")
    yl = lax.axis_index("yl")
    tok_count = tokens.shape[0]

    def up(v, axis="z", size=8):
        return lax.ppermute(v, axis, shift(size, 1))

    def down(v, axis="z", size=8):
        return lax.ppermute(v, axis, shift(size, -1))

    own_qkv = lax.all_gather(w_qkv.transpose(1, 0, 2), ROW, axis=1, tiled=True)

    w_out = jnp.concatenate([w_proj.T, w_down.T], axis=1)[None]
    piece = w_out.shape[1]
    half = piece // 2
    other_tokens, other_up, low, high = lax.optimization_barrier(
        (lax.ppermute(tokens, "yl", SWAP), across(w_up), up(w_out), down(w_out))
    )
    up_pair = both_rows(w_up, other_up)
    up_all = lax.all_gather(up_pair, ROW, axis=1, tiled=True).reshape(-1, w_up.shape[1])
    shards = [([(0, 0, 0)], w_out), ([(0, -1, 0)], low), ([(0, 1, 0)], high)]

    first = jnp.where(yl == 0, tokens, other_tokens)
    second = jnp.where(yl == 0, other_tokens, tokens)
    pair = jnp.stack([first, second])
    quarter = own_qkv.shape[1] // 2
    mine = lax.dynamic_slice_in_dim(own_qkv, c * quarter, quarter, axis=1)
    right, left, low, high, near, mine = lax.optimization_barrier(
        (
            up(pair, "x", 4),
            down(pair, "x", 4),
            up(low),
            down(high),
            across(jnp.concatenate([low, w_out, high])),
            mine,
        )
    )
    other_c = across(mine)
    other_d = lax.ppermute(other_c, "c", SWAP)
    shards += [([(0, -2, 0)], low), ([(0, 2, 0)], high)]
    shards += [([(1, -1, 0), (1, 0, 0), (1, 1, 0)], near)]

    middle = tok_count // 2
    far_a, far_b, low, high, near = lax.optimization_barrier(
        (
            up(right[:, :middle], "x", 4),
            down(left[:, middle:], "x", 4),
            up(low),
            down(high),
            near,
        )
    )
    shards += [([(0, -3, 0)], low), ([(0, 3, 0)], high)]
    end_a, end_b = up(low[:, :half]), down(high[:, half:])
    other_low, other_high = up(near[:1]), down(near[2:])
    shards += [([(0, 4, 0)], end_a), ([(0, 4, half)], end_b)]
    shards += [([(1, -2, 0)], other_low), ([(1, 2, 0)], other_high)]

    far = jnp.concatenate([far_a, far_b], axis=1)
    panels = place_tokens([pair, right, far, left])
    normed = layer_norm(panels.astype(jnp.float32), ln_gain).astype(jnp.bfloat16)

    base = (1 - yh) * 2 * quarter
    starts = jnp.stack([yh * 2 * quarter, base + c * quarter, base + (1 - c) * quarter])
    distant = jnp.concatenate([low, jnp.concatenate([end_a, end_b], axis=1), high])
    normed = tie(normed, (distant, other_low, other_high))
    distant = across(tie(distant, other_d))
    shards += [([(1, -3, 0), (1, 4, 0), (1, 3, 0)], distant)]
    attended = attention(starts, normed, own_qkv, other_c, other_d, q_gain, k_gain)
    activated = up_gelu(tie(normed, (attended, distant)), up_all)

    place = jnp.stack([yh, z])
    swapped = (lax.ppermute(attended, "c", SWAP), lax.ppermute(activated, "c", SWAP))
    mine = out_terms(place, piece, attended, activated, shards)
    theirs = out_terms(place, piece, *tie(swapped, mine), shards)
    mine, theirs = scatter_end(*scatter_start(mine, theirs))
    mine = mine.reshape(2, 1, piece, tok_count)
    theirs = theirs.reshape(2, 1, piece, tok_count)
    even = jnp.where(c == 0, mine, theirs)
    odd = jnp.where(c == 0, theirs, mine)
    branches = jnp.concatenate([even, odd], axis=1).reshape(4 * piece, tok_count)
    return (tokens.astype(jnp.float32) + branches.T).astype(jnp.bfloat16)


def solution(mesh):
    fine = Mesh(mesh.devices.reshape(2, 8, 2, 2, 4), ("yh", "z", "c", "yl", "x"))
    return jax.shard_map(
        local,
        mesh=fine,
        in_specs=(
            P(FSDP, MP),
            P(),
            P(FSDP, None, MP),
            P(FSDP, MP),
            P(MP, None),
            P(MP, None),
            P(MP, FSDP),
            P(MP, FSDP),
        ),
        out_specs=P(FSDP, MP),
        check_vma=False,
    )
```

```python
import functools

import jax
import jax.numpy as jnp
from jax import lax
from jax.experimental import pallas as pl
from jax.experimental.pallas import tpu as pltpu
from jax.sharding import Mesh, PartitionSpec as P

HD = 128
PATCHES = 256
FSDP = ("yh", "z", "c")
MP = ("yl", "x")
ROW = ("z", "c")
SWAP = [(0, 1), (1, 0)]


def layer_norm(values, gain):
    mean = jnp.mean(values, axis=-1, keepdims=True)
    centred = values - mean
    variance = jnp.mean(centred * centred, axis=-1, keepdims=True)
    return centred * lax.rsqrt(variance + 1e-06) * gain


def shift(n, k):
    return [(i, (i + k) % n) for i in range(n)]


def tie(values, *after):
    return lax.optimization_barrier((values, *after))[0]


def norm_kernel(x_ref, gain_ref, pair_ref, right_ref, left_ref, far_a_ref, far_b_ref, out_ref):
    panels = [(0, 0, pair_ref.at[0]), (1, 0, pair_ref.at[1])]
    panels += [(0, 1, right_ref.at[0]), (1, 1, right_ref.at[1])]
    panels += [(0, 2, far_a_ref), (1, 2, far_b_ref)]
    panels += [(0, 3, left_ref.at[0]), (1, 3, left_ref.at[1])]
    width = out_ref.shape[1] // len(panels)

    def mean(fn):
        total = sum(fn(ref[...].astype(jnp.float32)) for _, _, ref in panels)
        return jnp.sum(total, axis=-1, keepdims=True) / out_ref.shape[1]

    centre = mean(lambda v: v)
    scale = lax.rsqrt(mean(lambda v: (v - centre) * (v - centre)) + 1e-06)
    for h, k, ref in panels:
        at = h * 4 + lax.rem(x_ref[0] + 4 - k, 4)
        cols = pl.ds(pl.multiple_of(at * width, HD), width)
        values = (ref[...].astype(jnp.float32) - centre) * scale * gain_ref[:, cols]
        out_ref[:, cols] = values.astype(out_ref.dtype)


def norm_tokens(x, gain, pair, right, left, far_a, far_b):
    rows, width = far_a.shape
    tile = 128
    one = pl.BlockSpec((tile, width), lambda i: (i, 0))
    two = pl.BlockSpec((2, tile, width), lambda i: (0, i, 0))
    return pl.pallas_call(
        norm_kernel,
        grid=(rows // tile,),
        in_specs=[
            pl.BlockSpec(memory_space=pltpu.SMEM),
            pl.BlockSpec((1, 8 * width), lambda i: (0, 0)),
            two,
            two,
            two,
            one,
            one,
        ],
        out_specs=pl.BlockSpec((tile, 8 * width), lambda i: (i, 0)),
        out_shape=jax.ShapeDtypeStruct((rows, 8 * width), jnp.bfloat16),
        compiler_params=pltpu.CompilerParams(vmem_limit_bytes=32 * 2**20),
    )(x[None], gain[None], pair, right, left, far_a, far_b)


def both_rows(mine, other):
    yh = lax.axis_index("yh")
    return jnp.where(yh == 0, jnp.stack([mine, other]), jnp.stack([other, mine]))


def pick(blocks, at, axis):
    return lax.dynamic_index_in_dim(blocks, at, axis, keepdims=False)


def to_peers_x(blocks, axis):
    x = lax.axis_index("x")
    return [
        lax.ppermute(pick(blocks, (x + k) % 4, axis), "x", shift(4, k)) for k in (2, 1, 3)
    ]


def scatter_start(mine, theirs):
    yl, x = lax.axis_index("yl"), lax.axis_index("x")
    shape = (2, 4, mine.shape[0] // 8 * mine.shape[1], mine.shape[2])
    mine, theirs = mine.reshape(shape), theirs.reshape(shape)
    over_x = to_peers_x(mine, 1)
    both = [(core * 2 + at, (1 - core) * 2 + 1 - at) for core in range(2) for at in range(2)]
    over_y = lax.ppermute(pick(theirs, 1 - yl, 0), ("c", "yl"), both)
    kept = lax.ppermute(pick(theirs, yl, 0), "c", SWAP)
    over_x = tie(over_x, kept)
    return [pick(mine, x, 1)] + over_x, [kept, over_y]


def scatter_end(over_x, over_y):
    yl, x = lax.axis_index("yl"), lax.axis_index("x")

    def total(values):
        return sum(v.astype(jnp.float32) for v in values)

    by_y, by_x = total(over_x), total(over_y)
    other = lax.ppermute(pick(by_y, 1 - yl, 0).astype(jnp.bfloat16), "yl", SWAP)
    others = to_peers_x(by_x.astype(jnp.bfloat16), 0)
    return total([pick(by_y, yl, 0), other]), total([pick(by_x, x, 0)] + others)


def across(v):
    return lax.ppermute(v, "yh", SWAP)


def up_kernel(x_ref, w_ref, out_ref):
    pre = jnp.dot(x_ref[...], w_ref[...], preferred_element_type=jnp.float32)
    out_ref[...] = (0.5 * pre * (1.0 + lax.erf(pre * 0.7071067811865476))).astype(out_ref.dtype)


def up_gelu(x, w):
    tile = 256
    rows, depth = x.shape
    hidden = w.shape[1]
    return pl.pallas_call(
        up_kernel,
        grid=(hidden // tile,),
        in_specs=[
            pl.BlockSpec((rows, depth), lambda i: (0, 0)),
            pl.BlockSpec((depth, tile), lambda i: (0, i)),
        ],
        out_specs=pl.BlockSpec((rows, tile), lambda i: (0, i)),
        out_shape=jax.ShapeDtypeStruct((rows, hidden), jnp.bfloat16),
        compiler_params=pltpu.CompilerParams(vmem_limit_bytes=53 * 2**20),
    )(x, w)


def attention_kernel(
    starts_ref, x_ref, own_ref, near_ref, far_ref, q_gain_ref, k_gain_ref, out_ref, proj_ref
):
    rows, heads = x_ref.shape[0], q_gain_ref.shape[0]
    pieces = (own_ref, near_ref, far_ref)
    for part in range(3):
        total = None
        for i, w_ref in enumerate(pieces):
            depth = w_ref.shape[1]
            at = pl.multiple_of(starts_ref[i], HD)
            term = jnp.dot(
                x_ref[:, pl.ds(at, depth)], w_ref[part], preferred_element_type=jnp.float32
            )
            total = term if total is None else total + term
        proj_ref[part] = total
    for h in range(heads):
        cols = slice(h * HD, (h + 1) * HD)
        q_gain, k_gain = q_gain_ref[h : h + 1, :], k_gain_ref[h : h + 1, :]
        for image in range(rows // PATCHES):
            at = slice(image * PATCHES, (image + 1) * PATCHES)
            queries = layer_norm(proj_ref[0, at, cols], q_gain).astype(jnp.bfloat16)
            keys = layer_norm(proj_ref[1, at, cols], k_gain).astype(jnp.bfloat16)
            values = proj_ref[2, at, cols].astype(jnp.bfloat16)
            scores = lax.dot_general(
                queries, keys, (((1,), (1,)), ((), ())), preferred_element_type=jnp.float32
            ) * HD ** (-0.5)
            scores = scores - jnp.max(scores, axis=-1, keepdims=True)
            weights = jnp.exp(scores)
            probs = (weights / jnp.sum(weights, axis=-1, keepdims=True)).astype(jnp.bfloat16)
            mixed = jnp.dot(probs, values, preferred_element_type=jnp.float32)
            out_ref[at, cols] = mixed.astype(jnp.bfloat16)


def attention(starts, x, own, near, far, q_gain, k_gain):
    rows, depth = x.shape
    cols = own.shape[2]
    vmem = pl.BlockSpec(memory_space=pltpu.VMEM)
    return pl.pallas_call(
        attention_kernel,
        in_specs=[pl.BlockSpec(memory_space=pltpu.SMEM)] + [vmem] * 6,
        out_specs=vmem,
        out_shape=jax.ShapeDtypeStruct((rows, cols), jnp.bfloat16),
        scratch_shapes=[pltpu.VMEM((3, rows, cols), jnp.float32)],
        compiler_params=pltpu.CompilerParams(vmem_limit_bytes=40 * 2**20),
    )(starts, x, own, near, far, q_gain, k_gain)


def out_kernel(places, rows, *refs):
    at_ref, attended_ref, activated_ref = refs[:3]
    shards = refs[3 : 3 + len(places)]
    out_ref, held, sem = refs[3 + len(places) :]
    yh, z = at_ref[0], at_ref[1]
    slots = list(dict.fromkeys(place[:2] for group in places for place in group))
    copies = [[] for _ in slots]
    count = 0
    for group, shard in zip(places, shards):
        for i, (other, offset, start) in enumerate(group):
            slot = slots.index((other, offset))
            at = pl.ds(slot * rows + start, shard.shape[1])
            copy = pltpu.make_async_copy(shard.at[i], held.at[at], sem.at[count])
            copy.start()
            copies[slot].append(copy)
            count += 1
    split = attended_ref.shape[1]
    contract = (((1,), (1,)), ((), ()))
    step = 4
    for first in range(0, len(slots), step):
        for slot in range(first, first + step):
            for copy in copies[slot]:
                copy.wait()
        at = slice(first * rows, (first + step) * rows)
        total = lax.dot_general(
            held[at, :split], attended_ref[...], contract, preferred_element_type=jnp.float32
        )
        total += lax.dot_general(
            held[at, split:], activated_ref[...], contract, preferred_element_type=jnp.float32
        )
        total = total.astype(out_ref.dtype)
        for i in range(step):
            other, offset = slots[first + i]
            owner = (1 - yh if other else yh) * 8 + lax.rem(z + offset + 8, 8)
            out_ref[owner] = total[i * rows : (i + 1) * rows]


def out_terms(place, rows, attended, activated, shards):
    places = tuple(places for places, _ in shards)
    tokens = attended.shape[0]
    width = attended.shape[1] + activated.shape[1]
    vmem = pl.BlockSpec(memory_space=pltpu.VMEM)
    return pl.pallas_call(
        functools.partial(out_kernel, places, rows),
        in_specs=[pl.BlockSpec(memory_space=pltpu.SMEM), vmem, vmem]
        + [pl.BlockSpec(memory_space=pltpu.HBM)] * len(places),
        out_specs=vmem,
        out_shape=jax.ShapeDtypeStruct((16, rows, tokens), jnp.bfloat16),
        scratch_shapes=[
            pltpu.VMEM((16 * rows, width), jnp.bfloat16),
            pltpu.SemaphoreType.DMA((sum(len(group) for group in places),)),
        ],
        compiler_params=pltpu.CompilerParams(vmem_limit_bytes=58 * 2**20),
        cost_estimate=pl.CostEstimate(
            flops=32 * rows * width * tokens, bytes_accessed=0, transcendentals=0
        ),
    )(place, attended, activated, *(arrays for _, arrays in shards))


def local(tokens, ln_gain, w_qkv, w_up, q_gain, k_gain, w_proj, w_down):
    yh, z, c = lax.axis_index("yh"), lax.axis_index("z"), lax.axis_index("c")
    yl = lax.axis_index("yl")
    tok_count = tokens.shape[0]

    def up(v, axis="z", size=8):
        return lax.ppermute(v, axis, shift(size, 1))

    def down(v, axis="z", size=8):
        return lax.ppermute(v, axis, shift(size, -1))

    own_qkv = lax.all_gather(w_qkv.transpose(1, 0, 2), ROW, axis=1, tiled=True)

    w_out = jnp.concatenate([w_proj.T, w_down.T], axis=1)[None]
    piece = w_out.shape[1]
    half = piece // 2
    other_tokens, other_up, low, high = lax.optimization_barrier(
        (lax.ppermute(tokens, "yl", SWAP), across(w_up), up(w_out), down(w_out))
    )
    up_pair = both_rows(w_up, other_up)
    up_all = lax.all_gather(up_pair, ROW, axis=1, tiled=True).reshape(-1, w_up.shape[1])
    shards = [([(0, 0, 0)], w_out), ([(0, -1, 0)], low), ([(0, 1, 0)], high)]

    first = jnp.where(yl == 0, tokens, other_tokens)
    second = jnp.where(yl == 0, other_tokens, tokens)
    pair = jnp.stack([first, second])
    quarter = own_qkv.shape[1] // 2
    near = across(jnp.concatenate([low, w_out, high]))
    low, high = up(low), down(high)
    mine = lax.dynamic_slice_in_dim(tie(own_qkv, (low, high)), c * quarter, quarter, axis=1)
    right, left, near, mine = lax.optimization_barrier(
        (up(pair, "x", 4), down(pair, "x", 4), near, mine)
    )
    other_c = across(mine)
    shards += [([(0, -2, 0)], low), ([(0, 2, 0)], high)]
    shards += [([(1, -1, 0), (1, 0, 0), (1, 1, 0)], near)]

    low, high = up(low), down(high)
    far_a, far_b = up(right[0], "x", 4), down(left[1], "x", 4)
    shards += [([(0, -3, 0)], low), ([(0, 3, 0)], high)]
    end_a, end_b = up(low[:, :half]), down(high[:, half:])
    other_low, other_high = tie((near[:1], near[2:]), (low, high))
    other_low, other_high = up(other_low), down(other_high)
    shards += [([(0, 4, 0)], end_a), ([(0, 4, half)], end_b)]
    shards += [([(1, -2, 0)], other_low), ([(1, 2, 0)], other_high)]
    other_c = tie(other_c, (far_a, far_b, end_a, end_b, other_low, other_high))
    other_d = lax.ppermute(other_c, "c", SWAP)

    normed = norm_tokens(lax.axis_index("x"), ln_gain, pair, right, left, far_a, far_b)

    base = (1 - yh) * 2 * quarter
    starts = jnp.stack([yh * 2 * quarter, base + c * quarter, base + (1 - c) * quarter])
    distant = jnp.concatenate([low, jnp.concatenate([end_a, end_b], axis=1), high])
    normed = tie(normed, (distant, other_low, other_high))
    distant = across(tie(distant, other_d))
    shards += [([(1, -3, 0), (1, 4, 0), (1, 3, 0)], distant)]
    attended = attention(starts, normed, own_qkv, other_c, other_d, q_gain, k_gain)
    activated = up_gelu(tie(normed, (attended, distant)), up_all)

    place = jnp.stack([yh, z])
    swapped = (lax.ppermute(attended, "c", SWAP), lax.ppermute(activated, "c", SWAP))
    mine = out_terms(place, piece, attended, activated, shards)
    theirs = out_terms(place, piece, *tie(swapped, mine), shards)
    mine, theirs = scatter_end(*scatter_start(mine, theirs))
    mine = mine.reshape(2, 1, piece, tok_count)
    theirs = theirs.reshape(2, 1, piece, tok_count)
    even = jnp.where(c == 0, mine, theirs)
    odd = jnp.where(c == 0, theirs, mine)
    branches = jnp.concatenate([even, odd], axis=1).reshape(4 * piece, tok_count)
    return (tokens.astype(jnp.float32) + branches.T).astype(jnp.bfloat16)


def solution(mesh):
    fine = Mesh(mesh.devices.reshape(2, 8, 2, 2, 4), ("yh", "z", "c", "yl", "x"))
    return jax.shard_map(
        local,
        mesh=fine,
        in_specs=(
            P(FSDP, MP),
            P(),
            P(FSDP, None, MP),
            P(FSDP, MP),
            P(MP, None),
            P(MP, None),
            P(MP, FSDP),
            P(MP, FSDP),
        ),
        out_specs=P(FSDP, MP),
        check_vma=False,
    )
```

```python
import functools

import jax
import jax.numpy as jnp
from jax import lax
from jax.experimental import pallas as pl
from jax.experimental.pallas import tpu as pltpu
from jax.sharding import Mesh, PartitionSpec as P

HD = 128
PATCHES = 256
FSDP = ("yh", "z", "c")
MP = ("yl", "x")
ROW = ("z", "c")
SWAP = [(0, 1), (1, 0)]


def layer_norm(values, gain):
    mean = jnp.mean(values, axis=-1, keepdims=True)
    centred = values - mean
    variance = jnp.mean(centred * centred, axis=-1, keepdims=True)
    return centred * lax.rsqrt(variance + 1e-06) * gain


def shift(n, k):
    return [(i, (i + k) % n) for i in range(n)]


def tie(values, *after):
    return lax.optimization_barrier((values, *after))[0]


def norm_kernel(x_ref, gain_ref, pair_ref, right_ref, left_ref, far_a_ref, far_b_ref, out_ref):
    panels = [(0, 0, pair_ref.at[0]), (1, 0, pair_ref.at[1])]
    panels += [(0, 1, right_ref.at[0]), (1, 1, right_ref.at[1])]
    panels += [(0, 2, far_a_ref), (1, 2, far_b_ref)]
    panels += [(0, 3, left_ref.at[0]), (1, 3, left_ref.at[1])]
    width = out_ref.shape[1] // len(panels)

    def mean(fn):
        total = sum(fn(ref[...].astype(jnp.float32)) for _, _, ref in panels)
        return jnp.sum(total, axis=-1, keepdims=True) / out_ref.shape[1]

    centre = mean(lambda v: v)
    scale = lax.rsqrt(mean(lambda v: (v - centre) * (v - centre)) + 1e-06)
    for h, k, ref in panels:
        at = h * 4 + lax.rem(x_ref[0] + 4 - k, 4)
        cols = pl.ds(pl.multiple_of(at * width, HD), width)
        values = (ref[...].astype(jnp.float32) - centre) * scale * gain_ref[:, cols]
        out_ref[:, cols] = values.astype(out_ref.dtype)


def norm_tokens(x, gain, pair, right, left, far_a, far_b):
    rows, width = far_a.shape
    tile = 128
    one = pl.BlockSpec((tile, width), lambda i: (i, 0))
    two = pl.BlockSpec((2, tile, width), lambda i: (0, i, 0))
    return pl.pallas_call(
        norm_kernel,
        grid=(rows // tile,),
        in_specs=[
            pl.BlockSpec(memory_space=pltpu.SMEM),
            pl.BlockSpec((1, 8 * width), lambda i: (0, 0)),
            two,
            two,
            two,
            one,
            one,
        ],
        out_specs=pl.BlockSpec((tile, 8 * width), lambda i: (i, 0)),
        out_shape=jax.ShapeDtypeStruct((rows, 8 * width), jnp.bfloat16),
        compiler_params=pltpu.CompilerParams(vmem_limit_bytes=32 * 2**20),
    )(x[None], gain[None], pair, right, left, far_a, far_b)


def both_rows(mine, other):
    yh = lax.axis_index("yh")
    return jnp.where(yh == 0, jnp.stack([mine, other]), jnp.stack([other, mine]))


def pick(blocks, at, axis):
    return lax.dynamic_index_in_dim(blocks, at, axis, keepdims=False)


def to_peers_x(blocks, axis):
    x = lax.axis_index("x")
    return [
        lax.ppermute(pick(blocks, (x + k) % 4, axis), "x", shift(4, k)) for k in (2, 1, 3)
    ]


def scatter_start(mine, theirs):
    yl, x = lax.axis_index("yl"), lax.axis_index("x")
    shape = (2, 4, mine.shape[0] // 8 * mine.shape[1], mine.shape[2])
    mine, theirs = mine.reshape(shape), theirs.reshape(shape)
    over_x = to_peers_x(mine, 1)
    both = [(core * 2 + at, (1 - core) * 2 + 1 - at) for core in range(2) for at in range(2)]
    over_y = lax.ppermute(pick(theirs, 1 - yl, 0), ("c", "yl"), both)
    kept = lax.ppermute(pick(theirs, yl, 0), "c", SWAP)
    over_x = tie(over_x, kept)
    return [pick(mine, x, 1)] + over_x, [kept, over_y]


def scatter_end(over_x, over_y):
    yl, x = lax.axis_index("yl"), lax.axis_index("x")

    def total(values):
        return sum(v.astype(jnp.float32) for v in values)

    by_y, by_x = total(over_x), total(over_y)
    other = lax.ppermute(pick(by_y, 1 - yl, 0).astype(jnp.bfloat16), "yl", SWAP)
    others = to_peers_x(by_x.astype(jnp.bfloat16), 0)
    return total([pick(by_y, yl, 0), other]), total([pick(by_x, x, 0)] + others)


def across(v):
    return lax.ppermute(v, "yh", SWAP)


def up_kernel(x_ref, w_ref, out_ref):
    pre = jnp.dot(x_ref[...], w_ref[...], preferred_element_type=jnp.float32)
    out_ref[...] = (0.5 * pre * (1.0 + lax.erf(pre * 0.7071067811865476))).astype(out_ref.dtype)


def up_gelu(x, w):
    tile = 512
    rows, depth = x.shape
    hidden = w.shape[1]
    return pl.pallas_call(
        up_kernel,
        grid=(hidden // tile,),
        in_specs=[
            pl.BlockSpec((rows, depth), lambda i: (0, 0)),
            pl.BlockSpec((depth, tile), lambda i: (0, i)),
        ],
        out_specs=pl.BlockSpec((rows, tile), lambda i: (0, i)),
        out_shape=jax.ShapeDtypeStruct((rows, hidden), jnp.bfloat16),
        compiler_params=pltpu.CompilerParams(vmem_limit_bytes=46 * 2**20),
    )(x, w)


def attention_kernel(
    starts_ref, x_ref, own_ref, near_ref, far_ref, q_gain_ref, k_gain_ref, out_ref, proj_ref
):
    rows, heads = x_ref.shape[0], q_gain_ref.shape[0]
    pieces = (own_ref, near_ref, far_ref)
    for part in range(3):
        total = None
        for i, w_ref in enumerate(pieces):
            depth = w_ref.shape[1]
            at = pl.multiple_of(starts_ref[i], HD)
            term = jnp.dot(
                x_ref[:, pl.ds(at, depth)], w_ref[part], preferred_element_type=jnp.float32
            )
            total = term if total is None else total + term
        proj_ref[part] = total
    for h in range(heads):
        cols = slice(h * HD, (h + 1) * HD)
        q_gain, k_gain = q_gain_ref[h : h + 1, :], k_gain_ref[h : h + 1, :]
        for image in range(rows // PATCHES):
            at = slice(image * PATCHES, (image + 1) * PATCHES)
            queries = layer_norm(proj_ref[0, at, cols], q_gain).astype(jnp.bfloat16)
            keys = layer_norm(proj_ref[1, at, cols], k_gain).astype(jnp.bfloat16)
            values = proj_ref[2, at, cols].astype(jnp.bfloat16)
            scores = lax.dot_general(
                queries, keys, (((1,), (1,)), ((), ())), preferred_element_type=jnp.float32
            ) * HD ** (-0.5)
            scores = scores - jnp.max(scores, axis=-1, keepdims=True)
            weights = jnp.exp(scores)
            probs = (weights / jnp.sum(weights, axis=-1, keepdims=True)).astype(jnp.bfloat16)
            mixed = jnp.dot(probs, values, preferred_element_type=jnp.float32)
            out_ref[at, cols] = mixed.astype(jnp.bfloat16)


def attention(starts, x, own, near, far, q_gain, k_gain):
    rows, depth = x.shape
    cols = own.shape[2]
    vmem = pl.BlockSpec(memory_space=pltpu.VMEM)
    return pl.pallas_call(
        attention_kernel,
        in_specs=[pl.BlockSpec(memory_space=pltpu.SMEM)] + [vmem] * 6,
        out_specs=vmem,
        out_shape=jax.ShapeDtypeStruct((rows, cols), jnp.bfloat16),
        scratch_shapes=[pltpu.VMEM((3, rows, cols), jnp.float32)],
        compiler_params=pltpu.CompilerParams(vmem_limit_bytes=40 * 2**20),
    )(starts, x, own, near, far, q_gain, k_gain)


def gather_kernel(places, slots, rows, *refs):
    out_ref = refs[-1]
    for group, ref in zip(places, refs):
        for i, (other, offset, start) in enumerate(group):
            at = slots.index((other, offset)) * rows + start
            out_ref[at : at + ref.shape[1]] = ref[i]


def side_by_side(rows, shards):
    places = tuple(places for places, _ in shards)
    slots = list(dict.fromkeys(place[:2] for group in places for place in group))
    width = shards[0][1].shape[2]
    vmem = pl.BlockSpec(memory_space=pltpu.VMEM)
    gathered = pl.pallas_call(
        functools.partial(gather_kernel, places, slots, rows),
        in_specs=[vmem] * len(shards),
        out_specs=vmem,
        out_shape=jax.ShapeDtypeStruct((16 * rows, width), jnp.bfloat16),
        compiler_params=pltpu.CompilerParams(vmem_limit_bytes=32 * 2**20),
    )(*(arrays for _, arrays in shards))
    return gathered, slots


def out_kernel(slots, at_ref, weights_ref, attended_ref, activated_ref, out_ref):
    yh, z = at_ref[0], at_ref[1]
    rows = out_ref.shape[1]
    split = attended_ref.shape[1]
    contract = (((1,), (1,)), ((), ()))
    step = 4
    for first in range(0, len(slots), step):
        at = slice(first * rows, (first + step) * rows)
        total = lax.dot_general(
            weights_ref[at, :split], attended_ref[...], contract, preferred_element_type=jnp.float32
        )
        total += lax.dot_general(
            weights_ref[at, split:], activated_ref[...], contract, preferred_element_type=jnp.float32
        )
        total = total.astype(out_ref.dtype)
        for i in range(step):
            other, offset = slots[first + i]
            owner = (1 - yh if other else yh) * 8 + lax.rem(z + offset + 8, 8)
            out_ref[owner] = total[i * rows : (i + 1) * rows]


def out_terms(place, slots, weights, attended, activated):
    rows = weights.shape[0] // 16
    tokens = attended.shape[0]
    vmem = pl.BlockSpec(memory_space=pltpu.VMEM)
    return pl.pallas_call(
        functools.partial(out_kernel, slots),
        in_specs=[pl.BlockSpec(memory_space=pltpu.SMEM), vmem, vmem, vmem],
        out_specs=vmem,
        out_shape=jax.ShapeDtypeStruct((16, rows, tokens), jnp.bfloat16),
        compiler_params=pltpu.CompilerParams(vmem_limit_bytes=32 * 2**20),
    )(place, weights, attended, activated)


def local(tokens, ln_gain, w_qkv, w_up, q_gain, k_gain, w_proj, w_down):
    yh, z, c = lax.axis_index("yh"), lax.axis_index("z"), lax.axis_index("c")
    yl = lax.axis_index("yl")
    tok_count = tokens.shape[0]

    def up(v, axis="z", size=8):
        return lax.ppermute(v, axis, shift(size, 1))

    def down(v, axis="z", size=8):
        return lax.ppermute(v, axis, shift(size, -1))

    own_qkv = lax.all_gather(w_qkv.transpose(1, 0, 2), ROW, axis=1, tiled=True)

    w_out = jnp.concatenate([w_proj.T, w_down.T], axis=1)[None]
    piece = w_out.shape[1]
    half = piece // 2
    other_tokens, other_up, low, high = lax.optimization_barrier(
        (lax.ppermute(tokens, "yl", SWAP), across(w_up), up(w_out), down(w_out))
    )
    up_pair = both_rows(w_up, other_up)
    up_all = lax.all_gather(up_pair, ROW, axis=1, tiled=True).reshape(-1, w_up.shape[1])
    shards = [([(0, 0, 0)], w_out), ([(0, -1, 0)], low), ([(0, 1, 0)], high)]

    first = jnp.where(yl == 0, tokens, other_tokens)
    second = jnp.where(yl == 0, other_tokens, tokens)
    pair = jnp.stack([first, second])
    quarter = own_qkv.shape[1] // 2
    near = across(jnp.concatenate([low, w_out, high]))
    low, high = up(low), down(high)
    mine = lax.dynamic_slice_in_dim(tie(own_qkv, (low, high)), c * quarter, quarter, axis=1)
    right, left, near, mine = lax.optimization_barrier(
        (up(pair, "x", 4), down(pair, "x", 4), near, mine)
    )
    other_c = across(mine)
    shards += [([(0, -2, 0)], low), ([(0, 2, 0)], high)]
    shards += [([(1, -1, 0), (1, 0, 0), (1, 1, 0)], near)]

    low, high = up(low), down(high)
    far_a, far_b = up(right[0], "x", 4), down(left[1], "x", 4)
    shards += [([(0, -3, 0)], low), ([(0, 3, 0)], high)]
    end_a, end_b = up(low[:, :half]), down(high[:, half:])
    other_low, other_high = tie((near[:1], near[2:]), (low, high))
    other_low, other_high = up(other_low), down(other_high)
    shards += [([(0, 4, 0)], end_a), ([(0, 4, half)], end_b)]
    shards += [([(1, -2, 0)], other_low), ([(1, 2, 0)], other_high)]
    other_c = tie(other_c, (far_a, far_b, end_a, end_b))
    other_d = lax.ppermute(other_c, "c", SWAP)

    normed = norm_tokens(lax.axis_index("x"), ln_gain, pair, right, left, far_a, far_b)

    base = (1 - yh) * 2 * quarter
    starts = jnp.stack([yh * 2 * quarter, base + c * quarter, base + (1 - c) * quarter])
    distant = jnp.concatenate([low, jnp.concatenate([end_a, end_b], axis=1), high])
    normed = tie(normed, (distant, other_low, other_high))
    distant = across(tie(distant, other_d))
    shards += [([(1, -3, 0), (1, 4, 0), (1, 3, 0)], distant)]
    attended = attention(starts, normed, own_qkv, other_c, other_d, q_gain, k_gain)
    weights, slots = side_by_side(piece, shards)
    activated = up_gelu(tie(normed, (attended, weights)), up_all)

    place = jnp.stack([yh, z])
    swapped = (lax.ppermute(attended, "c", SWAP), lax.ppermute(activated, "c", SWAP))
    mine = out_terms(place, slots, weights, attended, activated)
    theirs = out_terms(place, slots, weights, *tie(swapped, mine))
    mine, theirs = scatter_end(*scatter_start(mine, theirs))
    mine = mine.reshape(2, 1, piece, tok_count)
    theirs = theirs.reshape(2, 1, piece, tok_count)
    even = jnp.where(c == 0, mine, theirs)
    odd = jnp.where(c == 0, theirs, mine)
    branches = jnp.concatenate([even, odd], axis=1).reshape(4 * piece, tok_count)
    return (tokens.astype(jnp.float32) + branches.T).astype(jnp.bfloat16)


def solution(mesh):
    fine = Mesh(mesh.devices.reshape(2, 8, 2, 2, 4), ("yh", "z", "c", "yl", "x"))
    return jax.shard_map(
        local,
        mesh=fine,
        in_specs=(
            P(FSDP, MP),
            P(),
            P(FSDP, None, MP),
            P(FSDP, MP),
            P(MP, None),
            P(MP, None),
            P(MP, FSDP),
            P(MP, FSDP),
        ),
        out_specs=P(FSDP, MP),
        check_vma=False,
    )
```

```python
import functools

import jax
import jax.numpy as jnp
from jax import lax
from jax.experimental import pallas as pl
from jax.experimental.pallas import tpu as pltpu
from jax.sharding import Mesh, PartitionSpec as P

HD = 128
PATCHES = 256
FSDP = ("yh", "z", "c")
MP = ("yl", "x")
ROW = ("z", "c")
SWAP = [(0, 1), (1, 0)]


def layer_norm(values, gain):
    mean = jnp.mean(values, axis=-1, keepdims=True)
    centred = values - mean
    variance = jnp.mean(centred * centred, axis=-1, keepdims=True)
    return centred * lax.rsqrt(variance + 1e-06) * gain


def shift(n, k):
    return [(i, (i + k) % n) for i in range(n)]


def tie(values, *after):
    return lax.optimization_barrier((values, *after))[0]


def norm_kernel(x_ref, gain_ref, pair_ref, right_ref, left_ref, far_a_ref, far_b_ref, out_ref):
    panels = [(0, 0, pair_ref.at[0]), (1, 0, pair_ref.at[1])]
    panels += [(0, 1, right_ref.at[0]), (1, 1, right_ref.at[1])]
    panels += [(0, 2, far_a_ref), (1, 2, far_b_ref)]
    panels += [(0, 3, left_ref.at[0]), (1, 3, left_ref.at[1])]
    width = out_ref.shape[1] // len(panels)

    def mean(fn):
        total = sum(fn(ref[...].astype(jnp.float32)) for _, _, ref in panels)
        return jnp.sum(total, axis=-1, keepdims=True) / out_ref.shape[1]

    centre = mean(lambda v: v)
    scale = lax.rsqrt(mean(lambda v: (v - centre) * (v - centre)) + 1e-06)
    for h, k, ref in panels:
        at = h * 4 + lax.rem(x_ref[0] + 4 - k, 4)
        cols = pl.ds(pl.multiple_of(at * width, HD), width)
        values = (ref[...].astype(jnp.float32) - centre) * scale * gain_ref[:, cols]
        out_ref[:, cols] = values.astype(out_ref.dtype)


def norm_tokens(x, gain, pair, right, left, far_a, far_b):
    rows, width = far_a.shape
    tile = 128
    one = pl.BlockSpec((tile, width), lambda i: (i, 0))
    two = pl.BlockSpec((2, tile, width), lambda i: (0, i, 0))
    return pl.pallas_call(
        norm_kernel,
        grid=(rows // tile,),
        in_specs=[
            pl.BlockSpec(memory_space=pltpu.SMEM),
            pl.BlockSpec((1, 8 * width), lambda i: (0, 0)),
            two,
            two,
            two,
            one,
            one,
        ],
        out_specs=pl.BlockSpec((tile, 8 * width), lambda i: (i, 0)),
        out_shape=jax.ShapeDtypeStruct((rows, 8 * width), jnp.bfloat16),
        compiler_params=pltpu.CompilerParams(vmem_limit_bytes=32 * 2**20),
    )(x[None], gain[None], pair, right, left, far_a, far_b)


def both_rows(mine, other):
    yh = lax.axis_index("yh")
    return jnp.where(yh == 0, jnp.stack([mine, other]), jnp.stack([other, mine]))


def pick(blocks, at, axis):
    return lax.dynamic_index_in_dim(blocks, at, axis, keepdims=False)


def to_peers_x(blocks, axis):
    x = lax.axis_index("x")
    return [
        lax.ppermute(pick(blocks, (x + k) % 4, axis), "x", shift(4, k)) for k in (2, 1, 3)
    ]


def scatter_start(mine, theirs):
    yl, x = lax.axis_index("yl"), lax.axis_index("x")
    shape = (2, 4, mine.shape[0] // 8 * mine.shape[1], mine.shape[2])
    mine, theirs = mine.reshape(shape), theirs.reshape(shape)
    over_x = to_peers_x(mine, 1)
    both = [(core * 2 + at, (1 - core) * 2 + 1 - at) for core in range(2) for at in range(2)]
    over_y = lax.ppermute(pick(theirs, 1 - yl, 0), ("c", "yl"), both)
    kept = lax.ppermute(pick(theirs, yl, 0), "c", SWAP)
    over_x = tie(over_x, kept)
    return [pick(mine, x, 1)] + over_x, [kept, over_y]


def scatter_end(over_x, over_y):
    yl, x = lax.axis_index("yl"), lax.axis_index("x")

    def total(values):
        return sum(v.astype(jnp.float32) for v in values)

    by_x = total(over_y)
    rounded = by_x.astype(jnp.bfloat16)
    others = to_peers_x(rounded, 0)
    by_y = total(tie(over_x, rounded))
    other = lax.ppermute(pick(by_y, 1 - yl, 0).astype(jnp.bfloat16), "yl", SWAP)
    return total([pick(by_y, yl, 0), other]), total([pick(by_x, x, 0)] + others)


def across(v):
    return lax.ppermute(v, "yh", SWAP)


def up_kernel(x_ref, w_ref, out_ref):
    pre = jnp.dot(x_ref[...], w_ref[...], preferred_element_type=jnp.float32)
    out_ref[...] = (0.5 * pre * (1.0 + lax.erf(pre * 0.7071067811865476))).astype(out_ref.dtype)


def up_gelu(x, w):
    tile = 512
    rows, depth = x.shape
    hidden = w.shape[1]
    return pl.pallas_call(
        up_kernel,
        grid=(hidden // tile,),
        in_specs=[
            pl.BlockSpec((rows, depth), lambda i: (0, 0)),
            pl.BlockSpec((depth, tile), lambda i: (0, i)),
        ],
        out_specs=pl.BlockSpec((rows, tile), lambda i: (0, i)),
        out_shape=jax.ShapeDtypeStruct((rows, hidden), jnp.bfloat16),
        compiler_params=pltpu.CompilerParams(vmem_limit_bytes=46 * 2**20),
    )(x, w)


def attention_kernel(
    starts_ref, x_ref, own_ref, near_ref, far_ref, q_gain_ref, k_gain_ref, out_ref, proj_ref
):
    rows, heads = x_ref.shape[0], q_gain_ref.shape[0]
    pieces = (own_ref, near_ref, far_ref)
    for part in range(3):
        total = None
        for i, w_ref in enumerate(pieces):
            depth = w_ref.shape[1]
            at = pl.multiple_of(starts_ref[i], HD)
            term = jnp.dot(
                x_ref[:, pl.ds(at, depth)], w_ref[part], preferred_element_type=jnp.float32
            )
            total = term if total is None else total + term
        proj_ref[part] = total
    for h in range(heads):
        cols = slice(h * HD, (h + 1) * HD)
        q_gain, k_gain = q_gain_ref[h : h + 1, :], k_gain_ref[h : h + 1, :]
        for image in range(rows // PATCHES):
            at = slice(image * PATCHES, (image + 1) * PATCHES)
            queries = layer_norm(proj_ref[0, at, cols], q_gain).astype(jnp.bfloat16)
            keys = layer_norm(proj_ref[1, at, cols], k_gain).astype(jnp.bfloat16)
            values = proj_ref[2, at, cols].astype(jnp.bfloat16)
            scores = lax.dot_general(
                queries, keys, (((1,), (1,)), ((), ())), preferred_element_type=jnp.float32
            ) * HD ** (-0.5)
            scores = scores - jnp.max(scores, axis=-1, keepdims=True)
            weights = jnp.exp(scores)
            probs = (weights / jnp.sum(weights, axis=-1, keepdims=True)).astype(jnp.bfloat16)
            mixed = jnp.dot(probs, values, preferred_element_type=jnp.float32)
            out_ref[at, cols] = mixed.astype(jnp.bfloat16)


def attention(starts, x, own, near, far, q_gain, k_gain):
    rows, depth = x.shape
    cols = own.shape[2]
    vmem = pl.BlockSpec(memory_space=pltpu.VMEM)
    return pl.pallas_call(
        attention_kernel,
        in_specs=[pl.BlockSpec(memory_space=pltpu.SMEM)] + [vmem] * 6,
        out_specs=vmem,
        out_shape=jax.ShapeDtypeStruct((rows, cols), jnp.bfloat16),
        scratch_shapes=[pltpu.VMEM((3, rows, cols), jnp.float32)],
        compiler_params=pltpu.CompilerParams(vmem_limit_bytes=40 * 2**20),
    )(starts, x, own, near, far, q_gain, k_gain)


def gather_kernel(places, slots, rows, *refs):
    out_ref = refs[-1]
    for group, ref in zip(places, refs):
        for i, (other, offset, start) in enumerate(group):
            at = slots.index((other, offset)) * rows + start
            out_ref[at : at + ref.shape[1]] = ref[i]


def side_by_side(rows, shards):
    places = tuple(places for places, _ in shards)
    slots = list(dict.fromkeys(place[:2] for group in places for place in group))
    width = shards[0][1].shape[2]
    vmem = pl.BlockSpec(memory_space=pltpu.VMEM)
    gathered = pl.pallas_call(
        functools.partial(gather_kernel, places, slots, rows),
        in_specs=[vmem] * len(shards),
        out_specs=vmem,
        out_shape=jax.ShapeDtypeStruct((16 * rows, width), jnp.bfloat16),
        compiler_params=pltpu.CompilerParams(vmem_limit_bytes=32 * 2**20),
    )(*(arrays for _, arrays in shards))
    return gathered, slots


def out_kernel(slots, at_ref, weights_ref, attended_ref, activated_ref, out_ref):
    yh, z = at_ref[0], at_ref[1]
    rows = out_ref.shape[1]
    split = attended_ref.shape[1]
    contract = (((1,), (1,)), ((), ()))
    step = 4
    for first in range(0, len(slots), step):
        at = slice(first * rows, (first + step) * rows)
        total = lax.dot_general(
            weights_ref[at, :split], attended_ref[...], contract, preferred_element_type=jnp.float32
        )
        total += lax.dot_general(
            weights_ref[at, split:], activated_ref[...], contract, preferred_element_type=jnp.float32
        )
        total = total.astype(out_ref.dtype)
        for i in range(step):
            other, offset = slots[first + i]
            owner = (1 - yh if other else yh) * 8 + lax.rem(z + offset + 8, 8)
            out_ref[owner] = total[i * rows : (i + 1) * rows]


def out_terms(place, slots, weights, attended, activated):
    rows = weights.shape[0] // 16
    tokens = attended.shape[0]
    vmem = pl.BlockSpec(memory_space=pltpu.VMEM)
    return pl.pallas_call(
        functools.partial(out_kernel, slots),
        in_specs=[pl.BlockSpec(memory_space=pltpu.SMEM), vmem, vmem, vmem],
        out_specs=vmem,
        out_shape=jax.ShapeDtypeStruct((16, rows, tokens), jnp.bfloat16),
        compiler_params=pltpu.CompilerParams(vmem_limit_bytes=32 * 2**20),
    )(place, weights, attended, activated)


def local(tokens, ln_gain, w_qkv, w_up, q_gain, k_gain, w_proj, w_down):
    yh, z, c = lax.axis_index("yh"), lax.axis_index("z"), lax.axis_index("c")
    yl = lax.axis_index("yl")
    tok_count = tokens.shape[0]

    def up(v, axis="z", size=8):
        return lax.ppermute(v, axis, shift(size, 1))

    def down(v, axis="z", size=8):
        return lax.ppermute(v, axis, shift(size, -1))

    own_qkv = lax.all_gather(w_qkv.transpose(1, 0, 2), ROW, axis=1, tiled=True)

    w_out = jnp.concatenate([w_proj.T, w_down.T], axis=1)[None]
    piece = w_out.shape[1]
    half = piece // 2
    other_tokens, other_up, low, high = lax.optimization_barrier(
        (lax.ppermute(tokens, "yl", SWAP), across(w_up), up(w_out), down(w_out))
    )
    up_pair = both_rows(w_up, other_up)
    up_all = lax.all_gather(up_pair, ROW, axis=1, tiled=True).reshape(-1, w_up.shape[1])
    shards = [([(0, 0, 0)], w_out), ([(0, -1, 0)], low), ([(0, 1, 0)], high)]

    first = jnp.where(yl == 0, tokens, other_tokens)
    second = jnp.where(yl == 0, other_tokens, tokens)
    pair = jnp.stack([first, second])
    quarter = own_qkv.shape[1] // 2
    near = across(jnp.concatenate([low, w_out, high]))
    low, high = up(low), down(high)
    mine = lax.dynamic_slice_in_dim(tie(own_qkv, (low, high)), c * quarter, quarter, axis=1)
    right, left, near, mine = lax.optimization_barrier(
        (up(pair, "x", 4), down(pair, "x", 4), near, mine)
    )
    other_c = across(mine)
    shards += [([(0, -2, 0)], low), ([(0, 2, 0)], high)]
    shards += [([(1, -1, 0), (1, 0, 0), (1, 1, 0)], near)]

    low, high = up(low), down(high)
    far_a, far_b = up(right[0], "x", 4), down(left[1], "x", 4)
    shards += [([(0, -3, 0)], low), ([(0, 3, 0)], high)]
    end_a, end_b = up(low[:, :half]), down(high[:, half:])
    other_low, other_high = tie((near[:1], near[2:]), (low, high))
    other_low, other_high = up(other_low), down(other_high)
    shards += [([(0, 4, 0)], end_a), ([(0, 4, half)], end_b)]
    shards += [([(1, -2, 0)], other_low), ([(1, 2, 0)], other_high)]
    other_c = tie(other_c, (far_a, far_b, end_a, end_b))
    other_d = lax.ppermute(other_c, "c", SWAP)

    normed = norm_tokens(lax.axis_index("x"), ln_gain, pair, right, left, far_a, far_b)

    base = (1 - yh) * 2 * quarter
    starts = jnp.stack([yh * 2 * quarter, base + c * quarter, base + (1 - c) * quarter])
    distant = jnp.concatenate([low, jnp.concatenate([end_a, end_b], axis=1), high])
    normed = tie(normed, distant)
    distant, other_d = lax.optimization_barrier((distant, other_d))
    distant = across(distant)
    shards += [([(1, -3, 0), (1, 4, 0), (1, 3, 0)], distant)]
    attended = attention(starts, normed, own_qkv, other_c, other_d, q_gain, k_gain)
    shards = [(places, tie(arrays, attended)) for places, arrays in shards[-3:]] + shards[:-3]
    weights, slots = side_by_side(piece, shards)
    activated = up_gelu(tie(normed, (attended, weights)), up_all)

    place = jnp.stack([yh, z])
    swapped = (lax.ppermute(attended, "c", SWAP), lax.ppermute(activated, "c", SWAP))
    mine = out_terms(place, slots, weights, attended, activated)
    theirs = out_terms(place, slots, weights, *tie(swapped, mine))
    mine, theirs = scatter_end(*scatter_start(mine, theirs))
    mine = mine.reshape(2, 1, piece, tok_count)
    theirs = theirs.reshape(2, 1, piece, tok_count)
    even = jnp.where(c == 0, mine, theirs)
    odd = jnp.where(c == 0, theirs, mine)
    branches = jnp.concatenate([even, odd], axis=1).reshape(4 * piece, tok_count)
    return (tokens.astype(jnp.float32) + branches.T).astype(jnp.bfloat16)


def solution(mesh):
    fine = Mesh(mesh.devices.reshape(2, 8, 2, 2, 4), ("yh", "z", "c", "yl", "x"))
    return jax.shard_map(
        local,
        mesh=fine,
        in_specs=(
            P(FSDP, MP),
            P(),
            P(FSDP, None, MP),
            P(FSDP, MP),
            P(MP, None),
            P(MP, None),
            P(MP, FSDP),
            P(MP, FSDP),
        ),
        out_specs=P(FSDP, MP),
        check_vma=False,
    )
```

```python
import functools

import jax
import jax.numpy as jnp
from jax import lax
from jax.experimental import pallas as pl
from jax.experimental.pallas import tpu as pltpu
from jax.sharding import Mesh, PartitionSpec as P

HD = 128
PATCHES = 256
FSDP = ("yh", "z", "c")
MP = ("yl", "x")
ROW = ("z", "c")
SWAP = [(0, 1), (1, 0)]


def layer_norm(values, gain):
    mean = jnp.mean(values, axis=-1, keepdims=True)
    centred = values - mean
    variance = jnp.mean(centred * centred, axis=-1, keepdims=True)
    return centred * lax.rsqrt(variance + 1e-06) * gain


def shift(n, k):
    return [(i, (i + k) % n) for i in range(n)]


def tie(values, *after):
    return lax.optimization_barrier((values, *after))[0]


def norm_kernel(x_ref, gain_ref, pair_ref, right_ref, left_ref, far_a_ref, far_b_ref, out_ref):
    panels = [(0, 0, pair_ref.at[0]), (1, 0, pair_ref.at[1])]
    panels += [(0, 1, right_ref.at[0]), (1, 1, right_ref.at[1])]
    panels += [(0, 2, far_a_ref), (1, 2, far_b_ref)]
    panels += [(0, 3, left_ref.at[0]), (1, 3, left_ref.at[1])]
    width = out_ref.shape[1] // len(panels)

    def mean(fn):
        total = sum(fn(ref[...].astype(jnp.float32)) for _, _, ref in panels)
        return jnp.sum(total, axis=-1, keepdims=True) / out_ref.shape[1]

    centre = mean(lambda v: v)
    scale = lax.rsqrt(mean(lambda v: (v - centre) * (v - centre)) + 1e-06)
    for h, k, ref in panels:
        at = h * 4 + lax.rem(x_ref[0] + 4 - k, 4)
        cols = pl.ds(pl.multiple_of(at * width, HD), width)
        values = (ref[...].astype(jnp.float32) - centre) * scale * gain_ref[:, cols]
        out_ref[:, cols] = values.astype(out_ref.dtype)


def norm_tokens(x, gain, pair, right, left, far_a, far_b):
    rows, width = far_a.shape
    tile = 128
    one = pl.BlockSpec((tile, width), lambda i: (i, 0))
    two = pl.BlockSpec((2, tile, width), lambda i: (0, i, 0))
    return pl.pallas_call(
        norm_kernel,
        grid=(rows // tile,),
        in_specs=[
            pl.BlockSpec(memory_space=pltpu.SMEM),
            pl.BlockSpec((1, 8 * width), lambda i: (0, 0)),
            two,
            two,
            two,
            one,
            one,
        ],
        out_specs=pl.BlockSpec((tile, 8 * width), lambda i: (i, 0)),
        out_shape=jax.ShapeDtypeStruct((rows, 8 * width), jnp.bfloat16),
        compiler_params=pltpu.CompilerParams(vmem_limit_bytes=32 * 2**20),
    )(x[None], gain[None], pair, right, left, far_a, far_b)


def both_rows(mine, other):
    yh = lax.axis_index("yh")
    return jnp.where(yh == 0, jnp.stack([mine, other]), jnp.stack([other, mine]))


def pick(blocks, at, axis):
    return lax.dynamic_index_in_dim(blocks, at, axis, keepdims=False)


def to_peers_x(blocks, axis):
    x = lax.axis_index("x")
    return [
        lax.ppermute(pick(blocks, (x + k) % 4, axis), "x", shift(4, k)) for k in (2, 1, 3)
    ]


def scatter_start(mine, theirs):
    yl, x = lax.axis_index("yl"), lax.axis_index("x")
    shape = (2, 4, mine.shape[0] // 8 * mine.shape[1], mine.shape[2])
    mine, theirs = mine.reshape(shape), theirs.reshape(shape)
    over_x = to_peers_x(mine, 1)
    both = [(core * 2 + at, (1 - core) * 2 + 1 - at) for core in range(2) for at in range(2)]
    over_y = lax.ppermute(pick(theirs, 1 - yl, 0), ("c", "yl"), both)
    kept = lax.ppermute(pick(theirs, yl, 0), "c", SWAP)
    over_x = tie(over_x, kept)
    return [pick(mine, x, 1)] + over_x, [kept, over_y]


def scatter_end(over_x, over_y):
    yl, x = lax.axis_index("yl"), lax.axis_index("x")

    def total(values):
        return sum(v.astype(jnp.float32) for v in values)

    by_x = total(over_y)
    rounded = by_x.astype(jnp.bfloat16)
    others = to_peers_x(rounded, 0)
    by_y = total(tie(over_x, rounded))
    other = lax.ppermute(pick(by_y, 1 - yl, 0).astype(jnp.bfloat16), "yl", SWAP)
    return total([pick(by_y, yl, 0), other]), total([pick(by_x, x, 0)] + others)


def across(v):
    return lax.ppermute(v, "yh", SWAP)


def up_kernel(x_ref, w_ref, out_ref):
    pre = jnp.dot(x_ref[...], w_ref[...], preferred_element_type=jnp.float32)
    out_ref[...] = (0.5 * pre * (1.0 + lax.erf(pre * 0.7071067811865476))).astype(out_ref.dtype)


def up_gelu(x, w):
    tile = 512
    rows, depth = x.shape
    hidden = w.shape[1]
    return pl.pallas_call(
        up_kernel,
        grid=(hidden // tile,),
        in_specs=[
            pl.BlockSpec((rows, depth), lambda i: (0, 0)),
            pl.BlockSpec((depth, tile), lambda i: (0, i)),
        ],
        out_specs=pl.BlockSpec((rows, tile), lambda i: (0, i)),
        out_shape=jax.ShapeDtypeStruct((rows, hidden), jnp.bfloat16),
        compiler_params=pltpu.CompilerParams(vmem_limit_bytes=46 * 2**20),
    )(x, w)


def attention_kernel(
    starts_ref, x_ref, own_ref, near_ref, far_ref, q_gain_ref, k_gain_ref, out_ref, proj_ref
):
    rows, heads = x_ref.shape[0], q_gain_ref.shape[0]
    pieces = (own_ref, near_ref, far_ref)
    for part in range(3):
        total = None
        for i, w_ref in enumerate(pieces):
            depth = w_ref.shape[1]
            at = pl.multiple_of(starts_ref[i], HD)
            term = jnp.dot(
                x_ref[:, pl.ds(at, depth)], w_ref[part], preferred_element_type=jnp.float32
            )
            total = term if total is None else total + term
        proj_ref[part] = total
    for h in range(heads):
        cols = slice(h * HD, (h + 1) * HD)
        q_gain, k_gain = q_gain_ref[h : h + 1, :], k_gain_ref[h : h + 1, :]
        for image in range(rows // PATCHES):
            at = slice(image * PATCHES, (image + 1) * PATCHES)
            queries = layer_norm(proj_ref[0, at, cols], q_gain).astype(jnp.bfloat16)
            keys = layer_norm(proj_ref[1, at, cols], k_gain).astype(jnp.bfloat16)
            values = proj_ref[2, at, cols].astype(jnp.bfloat16)
            scores = lax.dot_general(
                queries, keys, (((1,), (1,)), ((), ())), preferred_element_type=jnp.float32
            ) * HD ** (-0.5)
            scores = scores - jnp.max(scores, axis=-1, keepdims=True)
            weights = jnp.exp(scores)
            probs = (weights / jnp.sum(weights, axis=-1, keepdims=True)).astype(jnp.bfloat16)
            mixed = jnp.dot(probs, values, preferred_element_type=jnp.float32)
            out_ref[at, cols] = mixed.astype(jnp.bfloat16)


def attention(starts, x, own, near, far, q_gain, k_gain):
    rows, depth = x.shape
    cols = own.shape[2]
    vmem = pl.BlockSpec(memory_space=pltpu.VMEM)
    return pl.pallas_call(
        attention_kernel,
        in_specs=[pl.BlockSpec(memory_space=pltpu.SMEM)] + [vmem] * 6,
        out_specs=vmem,
        out_shape=jax.ShapeDtypeStruct((rows, cols), jnp.bfloat16),
        scratch_shapes=[pltpu.VMEM((3, rows, cols), jnp.float32)],
        compiler_params=pltpu.CompilerParams(vmem_limit_bytes=40 * 2**20),
    )(starts, x, own, near, far, q_gain, k_gain)


def gather_kernel(places, slots, rows, *refs):
    out_ref = refs[-1]
    for group, ref in zip(places, refs):
        for i, (other, offset, start) in enumerate(group):
            at = slots.index((other, offset)) * rows + start
            out_ref[at : at + ref.shape[1]] = ref[i]


def side_by_side(rows, shards, count):
    places = tuple(places for places, _ in shards)
    slots = list(dict.fromkeys(place[:2] for group in places for place in group))
    width = shards[0][1].shape[2]
    vmem = pl.BlockSpec(memory_space=pltpu.VMEM)
    gathered = pl.pallas_call(
        functools.partial(gather_kernel, places, slots, rows),
        in_specs=[vmem] * len(shards),
        out_specs=vmem,
        out_shape=jax.ShapeDtypeStruct((count * rows, width), jnp.bfloat16),
        compiler_params=pltpu.CompilerParams(vmem_limit_bytes=32 * 2**20),
    )(*(arrays for _, arrays in shards))
    return gathered, slots


def out_kernel(slots, at_ref, weights_ref, low_ref, high_ref, distant_ref, attended_ref, activated_ref, out_ref):
    yh, z = at_ref[0], at_ref[1]
    rows = out_ref.shape[1]
    split = attended_ref.shape[1]
    contract = (((1,), (1,)), ((), ()))

    def put(block, slots):
        total = lax.dot_general(
            block[:, :split], attended_ref[...], contract, preferred_element_type=jnp.float32
        )
        total += lax.dot_general(
            block[:, split:], activated_ref[...], contract, preferred_element_type=jnp.float32
        )
        total = total.astype(out_ref.dtype)
        for i, (other, offset) in enumerate(slots):
            owner = (1 - yh if other else yh) * 8 + lax.rem(z + offset + 8, 8)
            out_ref[owner] = total[i * rows : (i + 1) * rows]

    early = weights_ref.shape[0] // rows
    step = 4
    for first in range(0, early, step):
        last = min(first + step, early)
        put(weights_ref[first * rows : last * rows], slots[first:last])
    put(jnp.concatenate([low_ref[0], high_ref[0], *distant_ref[...]]), slots[early:])


def out_terms(place, slots, weights, low, high, distant, attended, activated):
    rows = low.shape[1]
    tokens = attended.shape[0]
    vmem = pl.BlockSpec(memory_space=pltpu.VMEM)
    return pl.pallas_call(
        functools.partial(out_kernel, slots),
        in_specs=[pl.BlockSpec(memory_space=pltpu.SMEM)] + [vmem] * 6,
        out_specs=vmem,
        out_shape=jax.ShapeDtypeStruct((16, rows, tokens), jnp.bfloat16),
        compiler_params=pltpu.CompilerParams(vmem_limit_bytes=32 * 2**20),
    )(place, weights, low, high, distant, attended, activated)


def local(tokens, ln_gain, w_qkv, w_up, q_gain, k_gain, w_proj, w_down):
    yh, z, c = lax.axis_index("yh"), lax.axis_index("z"), lax.axis_index("c")
    yl = lax.axis_index("yl")
    tok_count = tokens.shape[0]

    def up(v, axis="z", size=8):
        return lax.ppermute(v, axis, shift(size, 1))

    def down(v, axis="z", size=8):
        return lax.ppermute(v, axis, shift(size, -1))

    own_qkv = lax.all_gather(w_qkv.transpose(1, 0, 2), ROW, axis=1, tiled=True)

    w_out = jnp.concatenate([w_proj.T, w_down.T], axis=1)[None]
    piece = w_out.shape[1]
    half = piece // 2
    other_tokens, other_up, low, high = lax.optimization_barrier(
        (lax.ppermute(tokens, "yl", SWAP), across(w_up), up(w_out), down(w_out))
    )
    up_pair = both_rows(w_up, other_up)
    up_all = lax.all_gather(up_pair, ROW, axis=1, tiled=True).reshape(-1, w_up.shape[1])
    shards = [([(0, 0, 0)], w_out), ([(0, -1, 0)], low), ([(0, 1, 0)], high)]

    first = jnp.where(yl == 0, tokens, other_tokens)
    second = jnp.where(yl == 0, other_tokens, tokens)
    pair = jnp.stack([first, second])
    quarter = own_qkv.shape[1] // 2
    near = across(jnp.concatenate([low, w_out, high]))
    low, high = up(low), down(high)
    mine = lax.dynamic_slice_in_dim(tie(own_qkv, (low, high)), c * quarter, quarter, axis=1)
    right, left, near, mine = lax.optimization_barrier(
        (up(pair, "x", 4), down(pair, "x", 4), near, mine)
    )
    other_c = across(mine)
    shards += [([(0, -2, 0)], low), ([(0, 2, 0)], high)]
    shards += [([(1, -1, 0), (1, 0, 0), (1, 1, 0)], near)]

    low, high = up(low), down(high)
    far_a, far_b = up(right[0], "x", 4), down(left[1], "x", 4)
    shards += [([(0, -3, 0)], low), ([(0, 3, 0)], high)]
    end_a, end_b = up(low[:, :half]), down(high[:, half:])
    shards += [([(0, 4, 0)], end_a), ([(0, 4, half)], end_b)]

    ends = tie((near[:1], near[2:]), (low, high))
    other_low, other_high = up(ends[0]), down(ends[1])

    normed = norm_tokens(lax.axis_index("x"), ln_gain, pair, right, left, far_a, far_b)
    other_c = tie(other_c, (normed, end_a, end_b))
    other_d = lax.ppermute(other_c, "c", SWAP)

    base = (1 - yh) * 2 * quarter
    starts = jnp.stack([yh * 2 * quarter, base + c * quarter, base + (1 - c) * quarter])
    distant = jnp.concatenate([low, jnp.concatenate([end_a, end_b], axis=1), high])
    distant = across(tie(distant, other_d))
    attended = attention(starts, normed, own_qkv, other_c, other_d, q_gain, k_gain)

    shards = [(places, tie(arrays, attended)) for places, arrays in shards]
    weights, slots = side_by_side(piece, shards, 11)
    slots += [(1, -2), (1, 2), (1, -3), (1, 4), (1, 3)]
    weights = (weights, other_low, other_high, distant)
    activated = up_gelu(tie(normed, (attended, weights)), up_all)

    place = jnp.stack([yh, z])
    swapped = (lax.ppermute(attended, "c", SWAP), lax.ppermute(activated, "c", SWAP))
    mine = out_terms(place, slots, *weights, attended, activated)
    theirs = out_terms(place, slots, *weights, *tie(swapped, mine))
    mine, theirs = scatter_end(*scatter_start(mine, theirs))
    mine = mine.reshape(2, 1, piece, tok_count)
    theirs = theirs.reshape(2, 1, piece, tok_count)
    even = jnp.where(c == 0, mine, theirs)
    odd = jnp.where(c == 0, theirs, mine)
    branches = jnp.concatenate([even, odd], axis=1).reshape(4 * piece, tok_count)
    return (tokens.astype(jnp.float32) + branches.T).astype(jnp.bfloat16)


def solution(mesh):
    fine = Mesh(mesh.devices.reshape(2, 8, 2, 2, 4), ("yh", "z", "c", "yl", "x"))
    return jax.shard_map(
        local,
        mesh=fine,
        in_specs=(
            P(FSDP, MP),
            P(),
            P(FSDP, None, MP),
            P(FSDP, MP),
            P(MP, None),
            P(MP, None),
            P(MP, FSDP),
            P(MP, FSDP),
        ),
        out_specs=P(FSDP, MP),
        check_vma=False,
    )
```

```python
import functools

import jax
import jax.numpy as jnp
from jax import lax
from jax.experimental import pallas as pl
from jax.experimental.pallas import tpu as pltpu
from jax.sharding import Mesh, PartitionSpec as P

HD = 128
PATCHES = 256
FSDP = ("yh", "z", "c")
MP = ("yl", "x")
ROW = ("z", "c")
SWAP = [(0, 1), (1, 0)]


def layer_norm(values, gain):
    mean = jnp.mean(values, axis=-1, keepdims=True)
    centred = values - mean
    variance = jnp.mean(centred * centred, axis=-1, keepdims=True)
    return centred * lax.rsqrt(variance + 1e-06) * gain


def shift(n, k):
    return [(i, (i + k) % n) for i in range(n)]


def tie(values, *after):
    return lax.optimization_barrier((values, *after))[0]


def norm_kernel(x_ref, gain_ref, pair_ref, right_ref, left_ref, far_a_ref, far_b_ref, out_ref):
    panels = [(0, 0, pair_ref.at[0]), (1, 0, pair_ref.at[1])]
    panels += [(0, 1, right_ref.at[0]), (1, 1, right_ref.at[1])]
    panels += [(0, 2, far_a_ref), (1, 2, far_b_ref)]
    panels += [(0, 3, left_ref.at[0]), (1, 3, left_ref.at[1])]
    width = out_ref.shape[1] // len(panels)

    def mean(fn):
        total = sum(fn(ref[...].astype(jnp.float32)) for _, _, ref in panels)
        return jnp.sum(total, axis=-1, keepdims=True) / out_ref.shape[1]

    centre = mean(lambda v: v)
    scale = lax.rsqrt(mean(lambda v: (v - centre) * (v - centre)) + 1e-06)
    for h, k, ref in panels:
        at = h * 4 + lax.rem(x_ref[0] + 4 - k, 4)
        cols = pl.ds(pl.multiple_of(at * width, HD), width)
        values = (ref[...].astype(jnp.float32) - centre) * scale * gain_ref[:, cols]
        out_ref[:, cols] = values.astype(out_ref.dtype)


def norm_tokens(x, gain, pair, right, left, far_a, far_b):
    rows, width = far_a.shape
    tile = 128
    one = pl.BlockSpec((tile, width), lambda i: (i, 0))
    two = pl.BlockSpec((2, tile, width), lambda i: (0, i, 0))
    return pl.pallas_call(
        norm_kernel,
        grid=(rows // tile,),
        in_specs=[
            pl.BlockSpec(memory_space=pltpu.SMEM),
            pl.BlockSpec((1, 8 * width), lambda i: (0, 0)),
            two,
            two,
            two,
            one,
            one,
        ],
        out_specs=pl.BlockSpec((tile, 8 * width), lambda i: (i, 0)),
        out_shape=jax.ShapeDtypeStruct((rows, 8 * width), jnp.bfloat16),
        compiler_params=pltpu.CompilerParams(vmem_limit_bytes=32 * 2**20),
    )(x[None], gain[None], pair, right, left, far_a, far_b)


def both_rows(mine, other):
    yh = lax.axis_index("yh")
    return jnp.where(yh == 0, jnp.stack([mine, other]), jnp.stack([other, mine]))


def pick(blocks, at, axis):
    return lax.dynamic_index_in_dim(blocks, at, axis, keepdims=False)


def to_peers_x(blocks, axis, hop=0):
    x = lax.axis_index("x")
    arrived = []
    for k in (2, 1, 3):
        perm = [
            (core * 4 + at, (core ^ hop) * 4 + (at + k) % 4) for core in range(2) for at in range(4)
        ]
        arrived.append(lax.ppermute(pick(blocks, (x + k) % 4, axis), ("c", "x"), perm))
    return arrived


def scatter_start(mine, theirs):
    yl, x = lax.axis_index("yl"), lax.axis_index("x")
    shape = (2, 4, mine.shape[0] // 8 * mine.shape[1], mine.shape[2])
    mine, theirs = mine.reshape(shape), theirs.reshape(shape)
    over_y = lax.ppermute(pick(mine, 1 - yl, 0), "yl", SWAP)
    kept = lax.ppermute(pick(theirs, x, 1), "c", SWAP)
    over_x = to_peers_x(theirs, 1, 1)
    over_y = tie(over_y, kept)
    return [pick(mine, yl, 0), over_y], [kept] + over_x


def scatter_end(over_y, over_x):
    yl, x = lax.axis_index("yl"), lax.axis_index("x")

    def total(values):
        return sum(v.astype(jnp.float32) for v in values)

    by_x = total(over_y)
    rounded = by_x.astype(jnp.bfloat16)
    others = to_peers_x(rounded, 0)
    by_y = total(tie(over_x, rounded))
    other = lax.ppermute(pick(by_y, 1 - yl, 0).astype(jnp.bfloat16), "yl", SWAP)
    return total([pick(by_x, x, 0)] + others), total([pick(by_y, yl, 0), other])


def across(v):
    return lax.ppermute(v, "yh", SWAP)


def up_kernel(x_ref, w_ref, out_ref):
    pre = jnp.dot(x_ref[...], w_ref[...], preferred_element_type=jnp.float32)
    out_ref[...] = (0.5 * pre * (1.0 + lax.erf(pre * 0.7071067811865476))).astype(out_ref.dtype)


def up_gelu(x, w):
    tile = 512
    rows, depth = x.shape
    hidden = w.shape[1]
    return pl.pallas_call(
        up_kernel,
        grid=(hidden // tile,),
        in_specs=[
            pl.BlockSpec((rows, depth), lambda i: (0, 0)),
            pl.BlockSpec((depth, tile), lambda i: (0, i)),
        ],
        out_specs=pl.BlockSpec((rows, tile), lambda i: (0, i)),
        out_shape=jax.ShapeDtypeStruct((rows, hidden), jnp.bfloat16),
        compiler_params=pltpu.CompilerParams(vmem_limit_bytes=46 * 2**20),
    )(x, w)


def attention_kernel(
    starts_ref, x_ref, own_ref, near_ref, far_ref, q_gain_ref, k_gain_ref, out_ref, proj_ref
):
    rows, heads = x_ref.shape[0], q_gain_ref.shape[0]
    pieces = (own_ref, near_ref, far_ref)
    for part in range(3):
        total = None
        for i, w_ref in enumerate(pieces):
            depth = w_ref.shape[1]
            at = pl.multiple_of(starts_ref[i], HD)
            term = jnp.dot(
                x_ref[:, pl.ds(at, depth)], w_ref[part], preferred_element_type=jnp.float32
            )
            total = term if total is None else total + term
        proj_ref[part] = total
    for h in range(heads):
        cols = slice(h * HD, (h + 1) * HD)
        q_gain, k_gain = q_gain_ref[h : h + 1, :], k_gain_ref[h : h + 1, :]
        for image in range(rows // PATCHES):
            at = slice(image * PATCHES, (image + 1) * PATCHES)
            queries = layer_norm(proj_ref[0, at, cols], q_gain).astype(jnp.bfloat16)
            keys = layer_norm(proj_ref[1, at, cols], k_gain).astype(jnp.bfloat16)
            values = proj_ref[2, at, cols].astype(jnp.bfloat16)
            scores = lax.dot_general(
                queries, keys, (((1,), (1,)), ((), ())), preferred_element_type=jnp.float32
            ) * HD ** (-0.5)
            scores = scores - jnp.max(scores, axis=-1, keepdims=True)
            weights = jnp.exp(scores)
            probs = (weights / jnp.sum(weights, axis=-1, keepdims=True)).astype(jnp.bfloat16)
            mixed = jnp.dot(probs, values, preferred_element_type=jnp.float32)
            out_ref[at, cols] = mixed.astype(jnp.bfloat16)


def attention(starts, x, own, near, far, q_gain, k_gain):
    rows, depth = x.shape
    cols = own.shape[2]
    vmem = pl.BlockSpec(memory_space=pltpu.VMEM)
    return pl.pallas_call(
        attention_kernel,
        in_specs=[pl.BlockSpec(memory_space=pltpu.SMEM)] + [vmem] * 6,
        out_specs=vmem,
        out_shape=jax.ShapeDtypeStruct((rows, cols), jnp.bfloat16),
        scratch_shapes=[pltpu.VMEM((3, rows, cols), jnp.float32)],
        compiler_params=pltpu.CompilerParams(vmem_limit_bytes=40 * 2**20),
    )(starts, x, own, near, far, q_gain, k_gain)


def gather_kernel(places, slots, rows, *refs):
    out_ref = refs[-1]
    for group, ref in zip(places, refs):
        for i, (other, offset, start) in enumerate(group):
            at = slots.index((other, offset)) * rows + start
            out_ref[at : at + ref.shape[1]] = ref[i]


def side_by_side(rows, shards, count):
    places = tuple(places for places, _ in shards)
    slots = list(dict.fromkeys(place[:2] for group in places for place in group))
    width = shards[0][1].shape[2]
    vmem = pl.BlockSpec(memory_space=pltpu.VMEM)
    gathered = pl.pallas_call(
        functools.partial(gather_kernel, places, slots, rows),
        in_specs=[vmem] * len(shards),
        out_specs=vmem,
        out_shape=jax.ShapeDtypeStruct((count * rows, width), jnp.bfloat16),
        compiler_params=pltpu.CompilerParams(vmem_limit_bytes=32 * 2**20),
    )(*(arrays for _, arrays in shards))
    return gathered, slots


def out_kernel(slots, at_ref, weights_ref, low_ref, high_ref, distant_ref, attended_ref, activated_ref, out_ref):
    yh, z = at_ref[0], at_ref[1]
    rows = out_ref.shape[1]
    split = attended_ref.shape[1]
    contract = (((1,), (1,)), ((), ()))

    def put(block, slots):
        total = lax.dot_general(
            block[:, :split], attended_ref[...], contract, preferred_element_type=jnp.float32
        )
        total += lax.dot_general(
            block[:, split:], activated_ref[...], contract, preferred_element_type=jnp.float32
        )
        total = total.astype(out_ref.dtype)
        for i, (other, offset) in enumerate(slots):
            owner = (1 - yh if other else yh) * 8 + lax.rem(z + offset + 8, 8)
            out_ref[owner] = total[i * rows : (i + 1) * rows]

    early = weights_ref.shape[0] // rows
    step = 4
    for first in range(0, early, step):
        last = min(first + step, early)
        put(weights_ref[first * rows : last * rows], slots[first:last])
    put(jnp.concatenate([low_ref[0], high_ref[0], *distant_ref[...]]), slots[early:])


def out_terms(place, slots, weights, low, high, distant, attended, activated):
    rows = low.shape[1]
    tokens = attended.shape[0]
    vmem = pl.BlockSpec(memory_space=pltpu.VMEM)
    return pl.pallas_call(
        functools.partial(out_kernel, slots),
        in_specs=[pl.BlockSpec(memory_space=pltpu.SMEM)] + [vmem] * 6,
        out_specs=vmem,
        out_shape=jax.ShapeDtypeStruct((16, rows, tokens), jnp.bfloat16),
        compiler_params=pltpu.CompilerParams(vmem_limit_bytes=32 * 2**20),
    )(place, weights, low, high, distant, attended, activated)


def local(tokens, ln_gain, w_qkv, w_up, q_gain, k_gain, w_proj, w_down):
    yh, z, c = lax.axis_index("yh"), lax.axis_index("z"), lax.axis_index("c")
    yl = lax.axis_index("yl")
    tok_count = tokens.shape[0]

    def up(v, axis="z", size=8):
        return lax.ppermute(v, axis, shift(size, 1))

    def down(v, axis="z", size=8):
        return lax.ppermute(v, axis, shift(size, -1))

    own_qkv = lax.all_gather(w_qkv.transpose(1, 0, 2), ROW, axis=1, tiled=True)

    w_out = jnp.concatenate([w_proj.T, w_down.T], axis=1)[None]
    piece = w_out.shape[1]
    half = piece // 2
    other_tokens, other_up, low, high = lax.optimization_barrier(
        (lax.ppermute(tokens, "yl", SWAP), across(w_up), up(w_out), down(w_out))
    )
    up_pair = both_rows(w_up, other_up)
    up_all = lax.all_gather(up_pair, ROW, axis=1, tiled=True).reshape(-1, w_up.shape[1])
    shards = [([(0, 0, 0)], w_out), ([(0, -1, 0)], low), ([(0, 1, 0)], high)]

    first = jnp.where(yl == 0, tokens, other_tokens)
    second = jnp.where(yl == 0, other_tokens, tokens)
    pair = jnp.stack([first, second])
    quarter = own_qkv.shape[1] // 2
    near = across(jnp.concatenate([low, w_out, high]))
    low, high = up(low), down(high)
    mine = lax.dynamic_slice_in_dim(tie(own_qkv, (low, high)), c * quarter, quarter, axis=1)
    right, left, near, mine = lax.optimization_barrier(
        (up(pair, "x", 4), down(pair, "x", 4), near, mine)
    )
    other_c = across(mine)
    shards += [([(0, -2, 0)], low), ([(0, 2, 0)], high)]
    shards += [([(1, -1, 0), (1, 0, 0), (1, 1, 0)], near)]

    low, high = up(low), down(high)
    far_a, far_b = up(right[0], "x", 4), down(left[1], "x", 4)
    shards += [([(0, -3, 0)], low), ([(0, 3, 0)], high)]
    end_a, end_b = up(low[:, :half]), down(high[:, half:])
    shards += [([(0, 4, 0)], end_a), ([(0, 4, half)], end_b)]

    ends = tie((near[:1], near[2:]), (low, high))
    other_low, other_high = up(ends[0]), down(ends[1])

    normed = norm_tokens(lax.axis_index("x"), ln_gain, pair, right, left, far_a, far_b)
    other_c = tie(other_c, (normed, end_a, end_b))
    other_d = lax.ppermute(other_c, "c", SWAP)

    base = (1 - yh) * 2 * quarter
    starts = jnp.stack([yh * 2 * quarter, base + c * quarter, base + (1 - c) * quarter])
    distant = jnp.concatenate([low, jnp.concatenate([end_a, end_b], axis=1), high])
    distant = across(tie(distant, other_d))
    attended = attention(starts, normed, own_qkv, other_c, other_d, q_gain, k_gain)

    shards = [(places, tie(arrays, attended)) for places, arrays in shards]
    weights, slots = side_by_side(piece, shards, 11)
    slots += [(1, -2), (1, 2), (1, -3), (1, 4), (1, 3)]
    weights = (weights, other_low, other_high, distant)
    activated = up_gelu(tie(normed, (attended, weights)), up_all)

    place = jnp.stack([yh, z])
    swapped = (lax.ppermute(attended, "c", SWAP), lax.ppermute(activated, "c", SWAP))
    mine = out_terms(place, slots, *weights, attended, activated)
    theirs = out_terms(place, slots, *weights, *tie(swapped, mine))
    mine, theirs = scatter_end(*scatter_start(mine, theirs))
    mine = mine.reshape(2, 1, piece, tok_count)
    theirs = theirs.reshape(2, 1, piece, tok_count)
    even = jnp.where(c == 0, mine, theirs)
    odd = jnp.where(c == 0, theirs, mine)
    branches = jnp.concatenate([even, odd], axis=1).reshape(4 * piece, tok_count)
    return (tokens.astype(jnp.float32) + branches.T).astype(jnp.bfloat16)


def solution(mesh):
    fine = Mesh(mesh.devices.reshape(2, 8, 2, 2, 4), ("yh", "z", "c", "yl", "x"))
    return jax.shard_map(
        local,
        mesh=fine,
        in_specs=(
            P(FSDP, MP),
            P(),
            P(FSDP, None, MP),
            P(FSDP, MP),
            P(MP, None),
            P(MP, None),
            P(MP, FSDP),
            P(MP, FSDP),
        ),
        out_specs=P(FSDP, MP),
        check_vma=False,
    )
```

```python
import functools

import jax
import jax.numpy as jnp
from jax import lax
from jax.experimental import pallas as pl
from jax.experimental.pallas import tpu as pltpu
from jax.sharding import Mesh, PartitionSpec as P

HD = 128
PATCHES = 256
FSDP = ("yh", "z", "c")
MP = ("yl", "x")
ROW = ("z", "c")
SWAP = [(0, 1), (1, 0)]


def layer_norm(values, gain):
    mean = jnp.mean(values, axis=-1, keepdims=True)
    centred = values - mean
    variance = jnp.mean(centred * centred, axis=-1, keepdims=True)
    return centred * lax.rsqrt(variance + 1e-06) * gain


def shift(n, k):
    return [(i, (i + k) % n) for i in range(n)]


def tie(values, *after):
    return lax.optimization_barrier((values, *after))[0]


def norm_kernel(x_ref, gain_ref, pair_ref, right_ref, left_ref, far_a_ref, far_b_ref, out_ref):
    panels = [(0, 0, pair_ref.at[0]), (1, 0, pair_ref.at[1])]
    panels += [(0, 1, right_ref.at[0]), (1, 1, right_ref.at[1])]
    panels += [(0, 2, far_a_ref), (1, 2, far_b_ref)]
    panels += [(0, 3, left_ref.at[0]), (1, 3, left_ref.at[1])]
    width = out_ref.shape[1] // len(panels)

    def mean(fn):
        total = sum(fn(ref[...].astype(jnp.float32)) for _, _, ref in panels)
        return jnp.sum(total, axis=-1, keepdims=True) / out_ref.shape[1]

    centre = mean(lambda v: v)
    scale = lax.rsqrt(mean(lambda v: (v - centre) * (v - centre)) + 1e-06)
    for h, k, ref in panels:
        at = h * 4 + lax.rem(x_ref[0] + 4 - k, 4)
        cols = pl.ds(pl.multiple_of(at * width, HD), width)
        values = (ref[...].astype(jnp.float32) - centre) * scale * gain_ref[:, cols]
        out_ref[:, cols] = values.astype(out_ref.dtype)


def norm_tokens(x, gain, pair, right, left, far_a, far_b):
    rows, width = far_a.shape
    tile = 128
    one = pl.BlockSpec((tile, width), lambda i: (i, 0))
    two = pl.BlockSpec((2, tile, width), lambda i: (0, i, 0))
    return pl.pallas_call(
        norm_kernel,
        grid=(rows // tile,),
        in_specs=[
            pl.BlockSpec(memory_space=pltpu.SMEM),
            pl.BlockSpec((1, 8 * width), lambda i: (0, 0)),
            two,
            two,
            two,
            one,
            one,
        ],
        out_specs=pl.BlockSpec((tile, 8 * width), lambda i: (i, 0)),
        out_shape=jax.ShapeDtypeStruct((rows, 8 * width), jnp.bfloat16),
        compiler_params=pltpu.CompilerParams(vmem_limit_bytes=32 * 2**20),
    )(x[None], gain[None], pair, right, left, far_a, far_b)


def both_rows(mine, other):
    yh = lax.axis_index("yh")
    return jnp.where(yh == 0, jnp.stack([mine, other]), jnp.stack([other, mine]))


def pick(blocks, at, axis):
    return lax.dynamic_index_in_dim(blocks, at, axis, keepdims=False)


def to_peers_x(blocks, axis, hop=0):
    x = lax.axis_index("x")
    arrived = []
    for k in (2, 1, 3):
        perm = [
            (core * 4 + at, (core ^ hop) * 4 + (at + k) % 4) for core in range(2) for at in range(4)
        ]
        arrived.append(lax.ppermute(pick(blocks, (x + k) % 4, axis), ("c", "x"), perm))
    return arrived


def scatter_start(mine, theirs):
    yl, x = lax.axis_index("yl"), lax.axis_index("x")
    shape = (2, 4, mine.shape[0] // 8 * mine.shape[1], mine.shape[2])
    mine, theirs = mine.reshape(shape), theirs.reshape(shape)
    over_y = lax.ppermute(pick(mine, 1 - yl, 0), "yl", SWAP)
    kept = lax.ppermute(pick(theirs, x, 1), "c", SWAP)
    over_x = to_peers_x(theirs, 1, 1)
    over_y = tie(over_y, kept)
    return [pick(mine, yl, 0), over_y], [kept] + over_x


def scatter_end(over_y, over_x):
    yl, x = lax.axis_index("yl"), lax.axis_index("x")

    def total(values):
        return sum(v.astype(jnp.float32) for v in values)

    by_x = total(over_y)
    rounded = by_x.astype(jnp.bfloat16)
    others = to_peers_x(rounded, 0)
    by_y = total(tie(over_x, rounded))
    other = lax.ppermute(pick(by_y, 1 - yl, 0).astype(jnp.bfloat16), "yl", SWAP)
    return total([pick(by_x, x, 0)] + others), total([pick(by_y, yl, 0), other])


def across(v):
    return lax.ppermute(v, "yh", SWAP)


def up_kernel(x_ref, w_ref, out_ref):
    pre = jnp.dot(x_ref[...], w_ref[...], preferred_element_type=jnp.float32)
    out_ref[...] = (0.5 * pre * (1.0 + lax.erf(pre * 0.7071067811865476))).astype(out_ref.dtype)


def up_gelu(x, w):
    tile = 512
    rows, depth = x.shape
    hidden = w.shape[1]
    return pl.pallas_call(
        up_kernel,
        grid=(hidden // tile,),
        in_specs=[
            pl.BlockSpec((rows, depth), lambda i: (0, 0)),
            pl.BlockSpec((depth, tile), lambda i: (0, i)),
        ],
        out_specs=pl.BlockSpec((rows, tile), lambda i: (0, i)),
        out_shape=jax.ShapeDtypeStruct((rows, hidden), jnp.bfloat16),
        compiler_params=pltpu.CompilerParams(vmem_limit_bytes=46 * 2**20),
    )(x, w)


def attention_kernel(
    starts_ref, x_ref, own_ref, near_ref, far_ref, q_gain_ref, k_gain_ref, out_ref, proj_ref
):
    rows, heads = x_ref.shape[0], q_gain_ref.shape[0]
    pieces = (own_ref, near_ref, far_ref)
    for part in range(3):
        total = None
        for i, w_ref in enumerate(pieces):
            depth = w_ref.shape[1]
            at = pl.multiple_of(starts_ref[i], HD)
            term = jnp.dot(
                x_ref[:, pl.ds(at, depth)], w_ref[part], preferred_element_type=jnp.float32
            )
            total = term if total is None else total + term
        proj_ref[part] = total
    for h in range(heads):
        cols = slice(h * HD, (h + 1) * HD)
        q_gain, k_gain = q_gain_ref[h : h + 1, :], k_gain_ref[h : h + 1, :]
        for image in range(rows // PATCHES):
            at = slice(image * PATCHES, (image + 1) * PATCHES)
            queries = layer_norm(proj_ref[0, at, cols], q_gain).astype(jnp.bfloat16)
            keys = layer_norm(proj_ref[1, at, cols], k_gain).astype(jnp.bfloat16)
            values = proj_ref[2, at, cols].astype(jnp.bfloat16)
            scores = lax.dot_general(
                queries, keys, (((1,), (1,)), ((), ())), preferred_element_type=jnp.float32
            ) * HD ** (-0.5)
            scores = scores - jnp.max(scores, axis=-1, keepdims=True)
            weights = jnp.exp(scores)
            probs = (weights / jnp.sum(weights, axis=-1, keepdims=True)).astype(jnp.bfloat16)
            mixed = jnp.dot(probs, values, preferred_element_type=jnp.float32)
            out_ref[at, cols] = mixed.astype(jnp.bfloat16)


def attention(starts, x, own, near, far, q_gain, k_gain):
    rows, depth = x.shape
    cols = own.shape[2]
    vmem = pl.BlockSpec(memory_space=pltpu.VMEM)
    return pl.pallas_call(
        attention_kernel,
        in_specs=[pl.BlockSpec(memory_space=pltpu.SMEM)] + [vmem] * 6,
        out_specs=vmem,
        out_shape=jax.ShapeDtypeStruct((rows, cols), jnp.bfloat16),
        scratch_shapes=[pltpu.VMEM((3, rows, cols), jnp.float32)],
        compiler_params=pltpu.CompilerParams(vmem_limit_bytes=40 * 2**20),
    )(starts, x, own, near, far, q_gain, k_gain)


def gather_kernel(places, slots, rows, *refs):
    out_ref = refs[-1]
    for group, ref in zip(places, refs):
        for i, (other, offset, start) in enumerate(group):
            at = slots.index((other, offset)) * rows + start
            out_ref[at : at + ref.shape[1]] = ref[i]


def side_by_side(rows, shards, count):
    places = tuple(places for places, _ in shards)
    slots = list(dict.fromkeys(place[:2] for group in places for place in group))
    width = shards[0][1].shape[2]
    vmem = pl.BlockSpec(memory_space=pltpu.VMEM)
    gathered = pl.pallas_call(
        functools.partial(gather_kernel, places, slots, rows),
        in_specs=[vmem] * len(shards),
        out_specs=vmem,
        out_shape=jax.ShapeDtypeStruct((count * rows, width), jnp.bfloat16),
        compiler_params=pltpu.CompilerParams(vmem_limit_bytes=32 * 2**20),
    )(*(arrays for _, arrays in shards))
    return gathered, slots


def out_kernel(slots, at_ref, weights_ref, low_ref, high_ref, distant_ref, attended_ref, activated_ref, out_ref):
    yh, z = at_ref[0], at_ref[1]
    rows = out_ref.shape[1]
    split = attended_ref.shape[1]
    contract = (((1,), (1,)), ((), ()))

    def put(block, slots):
        total = lax.dot_general(
            block[:, :split], attended_ref[...], contract, preferred_element_type=jnp.float32
        )
        total += lax.dot_general(
            block[:, split:], activated_ref[...], contract, preferred_element_type=jnp.float32
        )
        total = total.astype(out_ref.dtype)
        for i, (other, offset) in enumerate(slots):
            owner = (1 - yh if other else yh) * 8 + lax.rem(z + offset + 8, 8)
            out_ref[owner] = total[i * rows : (i + 1) * rows]

    early = weights_ref.shape[0] // rows
    step = 4
    for first in range(0, early, step):
        last = min(first + step, early)
        put(weights_ref[first * rows : last * rows], slots[first:last])
    put(jnp.concatenate([low_ref[0], high_ref[0], *distant_ref[...]]), slots[early:])


def out_terms(place, slots, weights, low, high, distant, attended, activated):
    rows = low.shape[1]
    tokens = attended.shape[0]
    vmem = pl.BlockSpec(memory_space=pltpu.VMEM)
    return pl.pallas_call(
        functools.partial(out_kernel, slots),
        in_specs=[pl.BlockSpec(memory_space=pltpu.SMEM)] + [vmem] * 6,
        out_specs=vmem,
        out_shape=jax.ShapeDtypeStruct((16, rows, tokens), jnp.bfloat16),
        compiler_params=pltpu.CompilerParams(vmem_limit_bytes=32 * 2**20),
    )(place, weights, low, high, distant, attended, activated)


def local(tokens, ln_gain, w_qkv, w_up, q_gain, k_gain, w_proj, w_down):
    yh, z, c = lax.axis_index("yh"), lax.axis_index("z"), lax.axis_index("c")
    yl = lax.axis_index("yl")
    tok_count = tokens.shape[0]

    def up(v, axis="z", size=8):
        return lax.ppermute(v, axis, shift(size, 1))

    def down(v, axis="z", size=8):
        return lax.ppermute(v, axis, shift(size, -1))

    own_qkv = lax.all_gather(w_qkv.transpose(1, 0, 2), ROW, axis=1, tiled=True)

    w_out = jnp.concatenate([w_proj.T, w_down.T], axis=1)[None]
    piece = w_out.shape[1]
    half = piece // 2
    other_tokens, other_up, low, high = lax.optimization_barrier(
        (lax.ppermute(tokens, "yl", SWAP), across(w_up), up(w_out), down(w_out))
    )
    up_pair = both_rows(w_up, other_up)
    up_all = lax.all_gather(up_pair, ROW, axis=1, tiled=True).reshape(-1, w_up.shape[1])
    shards = [([(0, 0, 0)], w_out), ([(0, -1, 0)], low), ([(0, 1, 0)], high)]

    first = jnp.where(yl == 0, tokens, other_tokens)
    second = jnp.where(yl == 0, other_tokens, tokens)
    pair = jnp.stack([first, second])
    quarter = own_qkv.shape[1] // 2
    near = across(jnp.concatenate([low, w_out, high]))
    low, high = up(low), down(high)
    mine = lax.dynamic_slice_in_dim(tie(own_qkv, (low, high)), c * quarter, quarter, axis=1)
    right, left, near, mine = lax.optimization_barrier(
        (up(pair, "x", 4), down(pair, "x", 4), near, mine)
    )
    other_c = across(mine)
    shards += [([(0, -2, 0)], low), ([(0, 2, 0)], high)]
    shards += [([(1, -1, 0), (1, 0, 0), (1, 1, 0)], near)]

    low, high = up(low), down(high)
    far_a, far_b = up(right[0], "x", 4), down(left[1], "x", 4)
    shards += [([(0, -3, 0)], low), ([(0, 3, 0)], high)]
    end_a, end_b = up(low[:, :half]), down(high[:, half:])
    shards += [([(0, 4, 0)], end_a), ([(0, 4, half)], end_b)]

    ends = tie((near[:1], near[2:]), (low, high))
    other_low, other_high = up(ends[0]), down(ends[1])

    normed = norm_tokens(lax.axis_index("x"), ln_gain, pair, right, left, far_a, far_b)
    distant = jnp.concatenate([low, jnp.concatenate([end_a, end_b], axis=1), high])
    other_c, distant, normed = lax.optimization_barrier((other_c, distant, normed))
    other_d = lax.ppermute(other_c, "c", SWAP)
    distant = across(distant)

    base = (1 - yh) * 2 * quarter
    starts = jnp.stack([yh * 2 * quarter, base + c * quarter, base + (1 - c) * quarter])
    attended = attention(starts, normed, own_qkv, other_c, other_d, q_gain, k_gain)

    shards = [(places, tie(arrays, attended)) for places, arrays in shards]
    weights, slots = side_by_side(piece, shards, 11)
    slots += [(1, -2), (1, 2), (1, -3), (1, 4), (1, 3)]
    weights = (weights, other_low, other_high, distant)
    activated = up_gelu(tie(normed, (attended, weights)), up_all)

    place = jnp.stack([yh, z])
    swapped = (lax.ppermute(attended, "c", SWAP), lax.ppermute(activated, "c", SWAP))
    mine = out_terms(place, slots, *weights, attended, activated)
    theirs = out_terms(place, slots, *weights, *tie(swapped, mine))
    mine, theirs = scatter_end(*scatter_start(mine, theirs))
    mine = mine.reshape(2, 1, piece, tok_count)
    theirs = theirs.reshape(2, 1, piece, tok_count)
    even = jnp.where(c == 0, mine, theirs)
    odd = jnp.where(c == 0, theirs, mine)
    branches = jnp.concatenate([even, odd], axis=1).reshape(4 * piece, tok_count)
    return (tokens.astype(jnp.float32) + branches.T).astype(jnp.bfloat16)


def solution(mesh):
    fine = Mesh(mesh.devices.reshape(2, 8, 2, 2, 4), ("yh", "z", "c", "yl", "x"))
    return jax.shard_map(
        local,
        mesh=fine,
        in_specs=(
            P(FSDP, MP),
            P(),
            P(FSDP, None, MP),
            P(FSDP, MP),
            P(MP, None),
            P(MP, None),
            P(MP, FSDP),
            P(MP, FSDP),
        ),
        out_specs=P(FSDP, MP),
        check_vma=False,
    )
```
